32 devices in a mesh: grp: 2 (over x), seq: 16 (over z, y, core).
Axes of the slice: x: 2, y: 2, z: 4, core: 2. Of those that a mesh axis runs over, the one named last changes fastest.
Arguments:
- queries: bfloat16 [128, 5120], P(('grp', 'seq')), parts along dimension 0
- keys: bfloat16 [16384, 5120], P(('grp', 'seq')), parts along dimension 0
- values: bfloat16 [16384, 5120], P(('grp', 'seq')), parts along dimension 0, may hold values from -6 to 6
- gain: float32 [5120], replicated, may hold values from 0.1 to 1.9
Outputs:
- window_out: bfloat16 [128, 5120], P(('grp', 'seq')), parts along dimension 0
The draws below stay inside these ranges and needn't reach their ends.
There are 2 independent parts, one for each index of `grp`. The reference program is written for one: setup_inputs(seed, part) draws one part's arguments, and reference() takes and returns one part's arrays. A program takes and returns all parts, laid end to end along the dimension named above; an argument that names none is the same for every part. Nothing has to cross between parts.
All inputs are finite; a program needn't handle non-finite values.
Results may differ from the reference program's by a relative error of at most 0.001.
Values may be sent and summed in bfloat16 or wider, within the bound.
A program may use at most 128 MiB of HBM per device.

```python
import math
import jax
import jax.numpy as jnp
from jax import lax

HEADS = 40
HDIM = 128
HD = 5120
TOKENS = 8192
QW = 64


def base_keys(key):
    return jnp.clip(jax.random.normal(jax.random.fold_in(key, 11), (TOKENS, HD), jnp.float32), -6.0, 6.0)


def draw_keys(key, part):
    result = base_keys(key)
    return result.astype(jnp.bfloat16)


def draw_queries(key, part):
    result = 1.5 * jnp.clip(jax.random.normal(jax.random.fold_in(key, 17), (QW, HD), jnp.float32), -6.0, 6.0)
    return result.astype(jnp.bfloat16)


def levels(rng, shape, shards, smallest, largest):
    def one(position, blocks):
        steps = jax.random.uniform(jax.random.fold_in(jax.random.fold_in(rng, 6), position), (blocks,), jnp.float32, smallest / len(shards), largest / len(shards))
        return jnp.repeat(jnp.exp(steps), shape[position] // blocks).reshape((-1,) + (1,) * (len(shape) - position - 1))

    factor_of = one(*shards[0])
    for cut in shards[1:]:
        factor_of = factor_of * one(*cut)
    return factor_of


def normal_values(rng, dims, scale, bound, cuts=(), kind=jnp.bfloat16):
    values = jax.random.normal(rng, dims, jnp.float32) * scale
    if len(cuts) > 0:
        values = levels(rng, dims, cuts, -0.22, 0.18) * values
    return jnp.clip(values, min=-bound, max=bound).astype(kind)


def setup_inputs(seed: int = 0, part: int = 0) -> dict:
    key_list = jax.random.split(jax.random.key(seed), 5)
    part_keys = jax.random.split(jax.random.fold_in(key_list[4], part), 5)
    queries = draw_queries(jax.random.fold_in(jax.random.fold_in(key_list[4], part), 71), part)
    keys = draw_keys(jax.random.fold_in(jax.random.fold_in(key_list[4], part), 71), part)
    values = normal_values(part_keys[2], (TOKENS, HD), 1.0, 6.0, ((0, 16),))
    gain = jnp.clip(1.0 + 0.18 * jax.random.normal(key_list[3], (HD,), jnp.float32), 0.1, 1.9)
    return dict(queries=queries, keys=keys, values=values, gain=gain)


def reference(queries, keys, values, gain):
    score_scale = 1.0 / math.sqrt(HDIM)
    query_heads = queries.reshape(QW, HEADS, HDIM).transpose(1, 0, 2)
    key_heads = keys.reshape(TOKENS, HEADS, HDIM).transpose(1, 0, 2)
    value_heads = values.reshape(TOKENS, HEADS, HDIM).transpose(1, 0, 2)

    def one_head(members):
        query_head, key_head, value_head = members
        scores = jnp.dot(query_head, key_head.T, preferred_element_type=jnp.float32) * score_scale
        row_max = lax.optimization_barrier(jnp.max(scores, axis=1, keepdims=True))
        weights = jnp.exp(scores - row_max)
        denominator = lax.optimization_barrier(jnp.sum(weights, axis=1, keepdims=True))
        numerator = jnp.dot(weights, value_head.astype(jnp.float32), precision=lax.Precision.HIGHEST)
        return numerator / denominator
    attended = lax.map(one_head, (query_heads, key_heads, value_heads))
    attended = attended.transpose(1, 0, 2).reshape(QW, HEADS * HDIM)
    root_mean = jnp.sqrt(lax.optimization_barrier(jnp.mean(attended * attended, axis=1, keepdims=True)) + 1e-06)
    return (attended / root_mean * gain).astype(jnp.bfloat16)
```

```python
import functools
import math

import jax
import jax.numpy as jnp
from jax import lax
from jax.experimental import pallas as pl
from jax.experimental.pallas import tpu as pltpu
from jax.sharding import PartitionSpec as P

HDIM = 128
CHUNKS = (2, 4, 4)


def chunk_sizes(quads):
    if sum(CHUNKS) == quads:
        return CHUNKS
    return (quads,)


def remote(src, dst, send_sem, recv_sem, peer):
    return pltpu.make_async_remote_copy(
        src_ref=src,
        dst_ref=dst,
        send_sem=send_sem,
        recv_sem=recv_sem,
        device_id={"seq": peer},
        device_id_type=pl.DeviceIdType.MESH,
    )


def merge(left, right, out, pairs):
    width = pairs * HDIM
    slots = out.shape[0]
    rows = slots * 8
    stat_l = left[:, :, width:].reshape(rows, HDIM)
    stat_r = right[:, :, width:].reshape(rows, HDIM)
    peak = jnp.maximum(stat_l, stat_r)
    scale_l = jnp.exp2(stat_l - peak)
    scale_r = jnp.exp2(stat_r - peak)
    total = stat_l * pltpu.roll(scale_l, 64, 1) + stat_r * pltpu.roll(scale_r, 64, 1)
    column = lax.broadcasted_iota(jnp.int32, (rows, HDIM), 1)
    out[:, :, width:] = jnp.where(column < 64, peak, total).reshape(slots, 8, HDIM)
    for pair in range(pairs):
        at = pl.ds(pair * HDIM, HDIM)
        part_l = left[:, :, at].reshape(rows, HDIM) * scale_l[:, pair : pair + 1]
        part_r = right[:, :, at].reshape(rows, HDIM) * scale_r[:, pair : pair + 1]
        out[:, :, at] = (part_l + part_r).reshape(slots, 8, HDIM)


def kernel(n, sizes, q_ref, k_hbm, v_hbm, gain_ref, o_ref, *scratch):
    count = len(sizes)
    scratch = list(scratch)

    def take(many):
        taken = scratch[:many]
        del scratch[:many]
        return taken

    part, from_core, to_y, from_y, own, from_z = (take(count) for _ in range(6))
    k_buf, v_buf, packed, q_all, attended = take(5)
    kv_sem, gz_send, gz_recv, gy_send, gy_recv, gc_send, gc_recv = take(7)
    c_send, c_recv, y_send, y_recv, z_send, z_recv = take(6)

    nz = n // 4
    me = lax.axis_index("seq")
    z, y, core = me // 4, lax.rem(me // 2, 2), lax.rem(me, 2)
    sibling = z * 4 + y * 2 + (1 - core)
    across = z * 4 + (1 - y) * 2 + core
    offsets = list(range(1, nz))

    def z_peer(step):
        return lax.rem(z + step, nz)

    def device_at(zz):
        return zz * 4 + y * 2 + core

    starts = [sum(sizes[:i]) for i in range(count)]

    loads = []
    for i in range(count):
        columns = pl.ds(starts[i] * 4 * HDIM, sizes[i] * 4 * HDIM)
        pair = []
        for which, (hbm, buf) in enumerate(((k_hbm, k_buf), (v_hbm, v_buf))):
            copy = pltpu.make_async_copy(
                hbm.at[:, columns], buf.at[:, columns], kv_sem.at[i, which]
            )
            copy.start()
            pair.append(copy)
        loads.append(pair)

    barrier = pltpu.get_barrier_semaphore()
    for peer in [sibling, across] + [device_at(z_peer(s)) for s in offsets]:
        pl.semaphore_signal(
            barrier, inc=1, device_id={"seq": peer}, device_id_type=pl.DeviceIdType.MESH
        )

    quads = sum(sizes)
    mine = q_ref[...].astype(jnp.float32)
    for quad in range(quads):
        for j in range(4):
            head = quad * 4 + j
            packed[4 * j : 4 * j + 4, quad * HDIM : (quad + 1) * HDIM] = mine[
                :, head * HDIM : (head + 1) * HDIM
            ]
    base = core * (2 * nz) + y * nz
    other_base = core * (2 * nz) + (1 - y) * nz
    q_all[base + z] = packed[...].astype(jnp.bfloat16)

    pl.semaphore_wait(barrier, nz - 1 + 2)

    own_block = q_all.at[base + z]
    sends = []
    for s in offsets:
        to = z_peer(s)
        copy = remote(own_block, own_block, gz_send.at[to], gz_recv.at[z], device_at(to))
        copy.start()
        sends.append(copy)
    copy = remote(own_block, own_block, gy_send.at[z], gy_recv.at[z], across)
    copy.start()
    sends.append(copy)
    for s in offsets:
        src = z_peer(s)
        block = q_all.at[base + src]
        remote(block, block, gz_send.at[src], gz_recv.at[src], device_at(src)).wait_recv()
        copy = remote(block, block, gy_send.at[src], gy_recv.at[src], across)
        copy.start()
        sends.append(copy)
    near = q_all.at[pl.ds(base, nz)]
    copy = remote(near, near, gc_send.at[0], gc_recv.at[0], sibling)
    copy.start()
    sends.append(copy)
    for s in [0] + offsets:
        src = z_peer(s)
        block = q_all.at[other_base + src]
        remote(block, block, gy_send.at[src], gy_recv.at[src], across).wait_recv()
    far = q_all.at[pl.ds(other_base, nz)]
    copy = remote(far, far, gc_send.at[1], gc_recv.at[1], sibling)
    copy.start()
    sends.append(copy)
    sib_base = (1 - core) * (2 * nz)
    sib_near = q_all.at[pl.ds(sib_base + y * nz, nz)]
    sib_far = q_all.at[pl.ds(sib_base + (1 - y) * nz, nz)]
    remote(sib_near, sib_near, gc_send.at[0], gc_recv.at[0], sibling).wait_recv()
    remote(sib_far, sib_far, gc_send.at[1], gc_recv.at[1], sibling).wait_recv()

    rows = n * 8
    log_scale = math.log2(math.e) / math.sqrt(HDIM)
    first = lax.rem(lax.broadcasted_iota(jnp.int32, (rows, HDIM), 0), 8) < 4
    column = lax.broadcasted_iota(jnp.int32, (rows, HDIM), 1)

    def compute(i):
        for copy in loads[i]:
            copy.wait()
        width = sizes[i] * 2 * HDIM
        out = part[i]

        def quad_step(step, stats):
            quad = starts[i] + step
            q_quad = q_all[:, :, pl.ds(pl.multiple_of(quad * HDIM, HDIM), HDIM)].astype(jnp.float32)
            for half in range(2):
                q_pair = q_quad[:, 8 * half : 8 * half + 8, :].reshape(rows, HDIM)
                spread = jnp.concatenate(
                    [jnp.where(first, q_pair, 0.0), jnp.where(first, 0.0, q_pair)], axis=1
                ).astype(jnp.bfloat16)
                at = pl.ds(pl.multiple_of(quad * 4 * HDIM + half * 2 * HDIM, 2 * HDIM), 2 * HDIM)
                scores = lax.dot_general(
                    spread, k_buf[:, at], (((1,), (1,)), ((), ())),
                    preferred_element_type=jnp.float32,
                )
                peak = jnp.max(scores, axis=1, keepdims=True) * log_scale
                weights = jnp.exp2(scores * log_scale - peak)
                total = jnp.sum(weights, axis=1, keepdims=True)
                high = weights.astype(jnp.bfloat16)
                low = (weights - high.astype(jnp.float32)).astype(jnp.bfloat16)
                both = jnp.dot(
                    jnp.concatenate([high, low], axis=0), v_buf[:, at],
                    preferred_element_type=jnp.float32,
                )
                summed = both[:rows] + both[rows:]
                picked = jnp.where(first, summed[:, :HDIM], summed[:, HDIM:])
                pair = step * 2 + half
                out[:, :, pl.ds(pl.multiple_of(pair * HDIM, HDIM), HDIM)] = picked.reshape(n, 8, HDIM)
                stats = jnp.where(column == pair, peak, stats)
                stats = jnp.where(column == pair + 64, total, stats)
            return stats

        stats = lax.fori_loop(0, sizes[i], quad_step, jnp.zeros((rows, HDIM), jnp.float32))
        out[:, :, width:] = stats.reshape(n, 8, HDIM)

    def start_core(i):
        copy = remote(
            part[i].at[pl.ds((1 - core) * (2 * nz), 2 * nz)], from_core[i],
            c_send.at[i], c_recv.at[i], sibling,
        )
        copy.start()
        return copy

    def start_y(i, core_copy):
        core_copy.wait_recv()
        pairs = sizes[i] * 2
        merge(
            part[i].at[pl.ds(other_base, nz)], from_core[i].at[pl.ds((1 - y) * nz, nz)], to_y[i], pairs
        )
        copy = remote(to_y[i], from_y[i], y_send.at[i], y_recv.at[i], across)
        copy.start()
        merge(part[i].at[pl.ds(base, nz)], from_core[i].at[pl.ds(y * nz, nz)], own[i], pairs)
        return copy

    to_z = part

    def start_z(i, y_copy, core_copy):
        y_copy.wait_recv()
        core_copy.wait_send()
        there = (1 - core) * (2 * nz)
        merge(own[i], from_y[i], to_z[i].at[pl.ds(there, nz)], sizes[i] * 2)
        copies = []
        for s in offsets:
            to = z_peer(s)
            copy = remote(
                to_z[i].at[there + to], from_z[i].at[z], z_send.at[i, to], z_recv.at[i, z], device_at(to)
            )
            copy.start()
            copies.append(copy)
        from_z[i][z] = to_z[i][there + z]
        return copies

    def finish(i):
        pairs = sizes[i] * 2
        width = pairs * HDIM
        for s in offsets:
            src = z_peer(s)
            remote(
                from_z[i].at[src], from_z[i].at[src], z_send.at[i, src], z_recv.at[i, src], device_at(src)
            ).wait_recv()
        stats = from_z[i][:, :, width:]
        peak = jnp.max(stats, axis=0)
        scales = [jnp.exp2(stats[k] - peak) for k in range(nz)]
        total = sum(stats[k] * pltpu.roll(scales[k], 64, 1) for k in range(nz))
        squares = jnp.zeros((8, HDIM), jnp.float32)
        for pair in range(pairs):
            at = pl.ds(pair * HDIM, HDIM)
            numer = sum(from_z[i][k, :, at] * scales[k][:, pair : pair + 1] for k in range(nz))
            value = numer / total[:, 64 + pair : 65 + pair]
            attended[:, pl.ds((starts[i] * 2 + pair) * HDIM, HDIM)] = value
            squares = squares + value * value
        return squares

    core_copies, y_copies, z_copies = [], [], []
    for i in range(count + 2):
        if i < count:
            compute(i)
            core_copies.append(start_core(i))
        if 0 <= i - 1 < count:
            y_copies.append(start_y(i - 1, core_copies[i - 1]))
        if 0 <= i - 2 < count:
            z_copies.append(start_z(i - 2, y_copies[i - 2], core_copies[i - 2]))

    squares = sum(finish(i) for i in range(count))
    squares = squares + pltpu.roll(squares, 4, 0)
    mean = jnp.sum(squares, axis=1, keepdims=True) * (1.0 / o_ref.shape[1])
    inverse = 1.0 / jnp.sqrt(mean + 1e-06)
    for pair in range(quads * 2):
        value = attended[:, pair * HDIM : (pair + 1) * HDIM] * inverse
        for j in range(2):
            at = pl.ds((pair * 2 + j) * HDIM, HDIM)
            o_ref[:, at] = (value[4 * j : 4 * j + 4] * gain_ref[:, at]).astype(jnp.bfloat16)

    for copy in sends + y_copies:
        copy.wait_send()
    for copies in z_copies:
        for copy in copies:
            copy.wait_send()


def shards(n, queries, keys, values, gain):
    rows_here, width = queries.shape
    tokens = keys.shape[0]
    quads = width // (4 * HDIM)
    sizes = chunk_sizes(quads)
    count = len(sizes)
    nz = n // 4
    wides = [(2 * size + 1) * HDIM for size in sizes]

    def per_chunk(slots):
        return [pltpu.VMEM((slots, 8, wide), jnp.float32) for wide in wides]

    dma = pltpu.SemaphoreType.DMA
    scratch = (
        per_chunk(n) + per_chunk(n // 2) + per_chunk(nz) + per_chunk(nz) + per_chunk(nz) + per_chunk(nz)
        + [
            pltpu.VMEM((tokens, width), jnp.bfloat16),
            pltpu.VMEM((tokens, width), jnp.bfloat16),
            pltpu.VMEM((16, quads * HDIM), jnp.float32),
            pltpu.VMEM((n, 16, quads * HDIM), jnp.bfloat16),
            pltpu.VMEM((8, quads * 2 * HDIM), jnp.float32),
        ]
        + [dma((count, 2)), dma((nz,)), dma((nz,)), dma((nz,)), dma((nz,)), dma((2,)), dma((2,))]
        + [dma((count,)), dma((count,)), dma((count,)), dma((count,)), dma((count, nz)), dma((count, nz))]
    )
    vmem = pl.BlockSpec(memory_space=pltpu.VMEM)
    hbm = pl.BlockSpec(memory_space=pltpu.HBM)
    return pl.pallas_call(
        functools.partial(kernel, n, sizes),
        out_shape=jax.ShapeDtypeStruct((rows_here, width), jnp.bfloat16),
        in_specs=[vmem, hbm, hbm, vmem],
        out_specs=vmem,
        scratch_shapes=scratch,
        compiler_params=pltpu.CompilerParams(
            collective_id=0, has_side_effects=True, vmem_limit_bytes=56 * 1024 * 1024
        ),
    )(queries, keys, values, gain.reshape(1, width))


def solution(mesh):
    n = mesh.shape["seq"]
    in_specs = (P(("grp", "seq"), None), P(("grp", "seq"), None), P(("grp", "seq"), None), P())
    out_specs = P(("grp", "seq"), None)
    return jax.shard_map(
        functools.partial(shards, n), mesh=mesh, in_specs=in_specs, out_specs=out_specs, check_vma=False
    )
```

```python
import functools
import math

import jax
import jax.numpy as jnp
from jax import lax
from jax.experimental import pallas as pl
from jax.experimental.pallas import tpu as pltpu
from jax.sharding import PartitionSpec as P

HDIM = 128
CHUNKS = (2, 3, 3, 2)


def chunk_sizes(quads):
    if sum(CHUNKS) == quads:
        return CHUNKS
    return (quads,)


def remote(src, dst, send_sem, recv_sem, peer):
    return pltpu.make_async_remote_copy(
        src_ref=src,
        dst_ref=dst,
        send_sem=send_sem,
        recv_sem=recv_sem,
        device_id={"seq": peer},
        device_id_type=pl.DeviceIdType.MESH,
    )


def merge(left, right, out, pairs):
    width = pairs * HDIM
    slots = out.shape[0]
    rows = slots * 8
    stat_l = left[:, :, width:].reshape(rows, HDIM)
    stat_r = right[:, :, width:].reshape(rows, HDIM)
    peak = jnp.maximum(stat_l, stat_r)
    scale_l = jnp.exp2(stat_l - peak)
    scale_r = jnp.exp2(stat_r - peak)
    total = stat_l * pltpu.roll(scale_l, 64, 1) + stat_r * pltpu.roll(scale_r, 64, 1)
    column = lax.broadcasted_iota(jnp.int32, (rows, HDIM), 1)
    out[:, :, width:] = jnp.where(column < 64, peak, total).reshape(slots, 8, HDIM)
    for pair in range(pairs):
        at = pl.ds(pair * HDIM, HDIM)
        part_l = left[:, :, at].reshape(rows, HDIM) * scale_l[:, pair : pair + 1]
        part_r = right[:, :, at].reshape(rows, HDIM) * scale_r[:, pair : pair + 1]
        out[:, :, at] = (part_l + part_r).reshape(slots, 8, HDIM)


def kernel(n, sizes, q_ref, k_hbm, v_hbm, gain_ref, o_ref, *scratch):
    count = len(sizes)
    scratch = list(scratch)

    def take(many):
        taken = scratch[:many]
        del scratch[:many]
        return taken

    part, from_core, to_y, from_y, own, from_z = (take(count) for _ in range(6))
    k_buf, v_buf, packed, q_all, attended = take(5)
    kv_sem, gz_send, gz_recv, gy_send, gy_recv, gc_send, gc_recv = take(7)
    c_send, c_recv, y_send, y_recv, z_send, z_recv = take(6)

    nz = n // 4
    me = lax.axis_index("seq")
    z, y, core = me // 4, lax.rem(me // 2, 2), lax.rem(me, 2)
    sibling = z * 4 + y * 2 + (1 - core)
    across = z * 4 + (1 - y) * 2 + core
    offsets = list(range(1, nz))

    def z_peer(step):
        return lax.rem(z + step, nz)

    def device_at(zz):
        return zz * 4 + y * 2 + core

    starts = [sum(sizes[:i]) for i in range(count)]

    loads = []
    for i in range(count):
        columns = pl.ds(starts[i] * 4 * HDIM, sizes[i] * 4 * HDIM)
        pair = []
        for which, (hbm, buf) in enumerate(((k_hbm, k_buf), (v_hbm, v_buf))):
            copy = pltpu.make_async_copy(
                hbm.at[:, columns], buf.at[:, columns], kv_sem.at[i, which]
            )
            copy.start()
            pair.append(copy)
        loads.append(pair)

    barrier = pltpu.get_barrier_semaphore()
    for peer in [sibling, across] + [device_at(z_peer(s)) for s in offsets]:
        pl.semaphore_signal(
            barrier, inc=1, device_id={"seq": peer}, device_id_type=pl.DeviceIdType.MESH
        )

    quads = sum(sizes)
    mine = q_ref[...].astype(jnp.float32)
    for quad in range(quads):
        for j in range(4):
            head = quad * 4 + j
            packed[4 * j : 4 * j + 4, quad * HDIM : (quad + 1) * HDIM] = mine[
                :, head * HDIM : (head + 1) * HDIM
            ]
    base = core * (2 * nz) + y * nz
    other_base = core * (2 * nz) + (1 - y) * nz
    q_all[base + z] = packed[...].astype(jnp.bfloat16)

    pl.semaphore_wait(barrier, nz - 1 + 2)

    own_block = q_all.at[base + z]
    sends = []
    for s in offsets:
        to = z_peer(s)
        copy = remote(own_block, own_block, gz_send.at[to], gz_recv.at[z], device_at(to))
        copy.start()
        sends.append(copy)
    copy = remote(own_block, own_block, gy_send.at[z], gy_recv.at[z], across)
    copy.start()
    sends.append(copy)
    for s in offsets:
        src = z_peer(s)
        block = q_all.at[base + src]
        remote(block, block, gz_send.at[src], gz_recv.at[src], device_at(src)).wait_recv()
        copy = remote(block, block, gy_send.at[src], gy_recv.at[src], across)
        copy.start()
        sends.append(copy)
    near = q_all.at[pl.ds(base, nz)]
    copy = remote(near, near, gc_send.at[0], gc_recv.at[0], sibling)
    copy.start()
    sends.append(copy)
    for s in [0] + offsets:
        src = z_peer(s)
        block = q_all.at[other_base + src]
        remote(block, block, gy_send.at[src], gy_recv.at[src], across).wait_recv()
    far = q_all.at[pl.ds(other_base, nz)]
    copy = remote(far, far, gc_send.at[1], gc_recv.at[1], sibling)
    copy.start()
    sends.append(copy)
    sib_base = (1 - core) * (2 * nz)
    sib_near = q_all.at[pl.ds(sib_base + y * nz, nz)]
    sib_far = q_all.at[pl.ds(sib_base + (1 - y) * nz, nz)]
    remote(sib_near, sib_near, gc_send.at[0], gc_recv.at[0], sibling).wait_recv()
    remote(sib_far, sib_far, gc_send.at[1], gc_recv.at[1], sibling).wait_recv()

    rows = n * 8
    log_scale = math.log2(math.e) / math.sqrt(HDIM)
    first = lax.rem(lax.broadcasted_iota(jnp.int32, (rows, HDIM), 0), 8) < 4
    column = lax.broadcasted_iota(jnp.int32, (rows, HDIM), 1)

    def compute(i):
        for copy in loads[i]:
            copy.wait()
        width = sizes[i] * 2 * HDIM
        out = part[i]

        def quad_step(step, stats):
            quad = starts[i] + step
            q_quad = q_all[:, :, pl.ds(quad * HDIM, HDIM)].astype(jnp.float32)
            for half in range(2):
                q_pair = q_quad[:, 8 * half : 8 * half + 8, :].reshape(rows, HDIM)
                spread = jnp.concatenate(
                    [jnp.where(first, q_pair, 0.0), jnp.where(first, 0.0, q_pair)], axis=1
                ).astype(jnp.bfloat16)
                at = pl.ds((quad * 2 + half) * 2 * HDIM, 2 * HDIM)
                scores = lax.dot_general(
                    spread, k_buf[:, at], (((1,), (1,)), ((), ())),
                    preferred_element_type=jnp.float32,
                )
                peak = jnp.max(scores, axis=1, keepdims=True) * log_scale
                weights = jnp.exp2(scores * log_scale - peak)
                total = jnp.sum(weights, axis=1, keepdims=True)
                high = weights.astype(jnp.bfloat16)
                low = (weights - high.astype(jnp.float32)).astype(jnp.bfloat16)
                both = jnp.dot(
                    jnp.concatenate([high, low], axis=0), v_buf[:, at],
                    preferred_element_type=jnp.float32,
                )
                summed = both[:rows] + both[rows:]
                picked = jnp.where(first, summed[:, :HDIM], summed[:, HDIM:])
                pair = step * 2 + half
                out[:, :, pl.ds(pair * HDIM, HDIM)] = picked.reshape(n, 8, HDIM)
                stats = jnp.where(column == pair, peak, stats)
                stats = jnp.where(column == pair + 64, total, stats)
            return stats

        stats = jnp.zeros((rows, HDIM), jnp.float32)
        for step in range(sizes[i]):
            stats = quad_step(step, stats)
        out[:, :, width:] = stats.reshape(n, 8, HDIM)

    def start_core(i):
        copy = remote(
            part[i].at[pl.ds((1 - core) * (2 * nz), 2 * nz)], from_core[i],
            c_send.at[i], c_recv.at[i], sibling,
        )
        copy.start()
        return copy

    def start_y(i, core_copy):
        core_copy.wait_recv()
        pairs = sizes[i] * 2
        merge(
            part[i].at[pl.ds(other_base, nz)], from_core[i].at[pl.ds((1 - y) * nz, nz)], to_y[i], pairs
        )
        copy = remote(to_y[i], from_y[i], y_send.at[i], y_recv.at[i], across)
        copy.start()
        merge(part[i].at[pl.ds(base, nz)], from_core[i].at[pl.ds(y * nz, nz)], own[i], pairs)
        return copy

    to_z = part

    def start_z(i, y_copy, core_copy):
        y_copy.wait_recv()
        core_copy.wait_send()
        there = (1 - core) * (2 * nz)
        merge(own[i], from_y[i], to_z[i].at[pl.ds(there, nz)], sizes[i] * 2)
        copies = []
        for s in offsets:
            to = z_peer(s)
            copy = remote(
                to_z[i].at[there + to], from_z[i].at[z], z_send.at[i, to], z_recv.at[i, z], device_at(to)
            )
            copy.start()
            copies.append(copy)
        from_z[i][z] = to_z[i][there + z]
        return copies

    def finish(i):
        pairs = sizes[i] * 2
        width = pairs * HDIM
        for s in offsets:
            src = z_peer(s)
            remote(
                from_z[i].at[src], from_z[i].at[src], z_send.at[i, src], z_recv.at[i, src], device_at(src)
            ).wait_recv()
        stats = from_z[i][:, :, width:]
        peak = jnp.max(stats, axis=0)
        scales = [jnp.exp2(stats[k] - peak) for k in range(nz)]
        total = sum(stats[k] * pltpu.roll(scales[k], 64, 1) for k in range(nz))
        squares = jnp.zeros((8, HDIM), jnp.float32)
        for pair in range(pairs):
            at = pl.ds(pair * HDIM, HDIM)
            numer = sum(from_z[i][k, :, at] * scales[k][:, pair : pair + 1] for k in range(nz))
            value = numer / total[:, 64 + pair : 65 + pair]
            attended[:, pl.ds((starts[i] * 2 + pair) * HDIM, HDIM)] = value
            squares = squares + value * value
        return squares

    core_copies, y_copies, z_copies = [], [], []
    for i in range(count + 2):
        if i < count:
            compute(i)
            core_copies.append(start_core(i))
        if 0 <= i - 1 < count:
            y_copies.append(start_y(i - 1, core_copies[i - 1]))
        if 0 <= i - 2 < count:
            z_copies.append(start_z(i - 2, y_copies[i - 2], core_copies[i - 2]))

    squares = sum(finish(i) for i in range(count))
    squares = squares + pltpu.roll(squares, 4, 0)
    mean = jnp.sum(squares, axis=1, keepdims=True) * (1.0 / o_ref.shape[1])
    inverse = 1.0 / jnp.sqrt(mean + 1e-06)
    for pair in range(quads * 2):
        value = attended[:, pair * HDIM : (pair + 1) * HDIM] * inverse
        for j in range(2):
            at = pl.ds((pair * 2 + j) * HDIM, HDIM)
            o_ref[:, at] = (value[4 * j : 4 * j + 4] * gain_ref[:, at]).astype(jnp.bfloat16)

    for copy in sends + y_copies:
        copy.wait_send()
    for copies in z_copies:
        for copy in copies:
            copy.wait_send()


def shards(n, queries, keys, values, gain):
    rows_here, width = queries.shape
    tokens = keys.shape[0]
    quads = width // (4 * HDIM)
    sizes = chunk_sizes(quads)
    count = len(sizes)
    nz = n // 4
    wides = [(2 * size + 1) * HDIM for size in sizes]

    def per_chunk(slots):
        return [pltpu.VMEM((slots, 8, wide), jnp.float32) for wide in wides]

    dma = pltpu.SemaphoreType.DMA
    scratch = (
        per_chunk(n) + per_chunk(n // 2) + per_chunk(nz) + per_chunk(nz) + per_chunk(nz) + per_chunk(nz)
        + [
            pltpu.VMEM((tokens, width), jnp.bfloat16),
            pltpu.VMEM((tokens, width), jnp.bfloat16),
            pltpu.VMEM((16, quads * HDIM), jnp.float32),
            pltpu.VMEM((n, 16, quads * HDIM), jnp.bfloat16),
            pltpu.VMEM((8, quads * 2 * HDIM), jnp.float32),
        ]
        + [dma((count, 2)), dma((nz,)), dma((nz,)), dma((nz,)), dma((nz,)), dma((2,)), dma((2,))]
        + [dma((count,)), dma((count,)), dma((count,)), dma((count,)), dma((count, nz)), dma((count, nz))]
    )
    vmem = pl.BlockSpec(memory_space=pltpu.VMEM)
    hbm = pl.BlockSpec(memory_space=pltpu.HBM)
    return pl.pallas_call(
        functools.partial(kernel, n, sizes),
        out_shape=jax.ShapeDtypeStruct((rows_here, width), jnp.bfloat16),
        in_specs=[vmem, hbm, hbm, vmem],
        out_specs=vmem,
        scratch_shapes=scratch,
        compiler_params=pltpu.CompilerParams(
            collective_id=0, has_side_effects=True, vmem_limit_bytes=56 * 1024 * 1024
        ),
    )(queries, keys, values, gain.reshape(1, width))


def solution(mesh):
    n = mesh.shape["seq"]
    in_specs = (P(("grp", "seq"), None), P(("grp", "seq"), None), P(("grp", "seq"), None), P())
    out_specs = P(("grp", "seq"), None)
    return jax.shard_map(
        functools.partial(shards, n), mesh=mesh, in_specs=in_specs, out_specs=out_specs, check_vma=False
    )
```

```python
import functools
import math

import jax
import jax.numpy as jnp
from jax import lax
from jax.experimental import pallas as pl
from jax.experimental.pallas import tpu as pltpu
from jax.sharding import PartitionSpec as P

HDIM = 128
CHUNKS = (2, 3, 3, 2)


def chunk_sizes(quads):
    if sum(CHUNKS) == quads:
        return CHUNKS
    return (quads,)


def remote(src, dst, send_sem, recv_sem, peer):
    return pltpu.make_async_remote_copy(
        src_ref=src,
        dst_ref=dst,
        send_sem=send_sem,
        recv_sem=recv_sem,
        device_id={"seq": peer},
        device_id_type=pl.DeviceIdType.MESH,
    )


def merge(left, right, out, pairs):
    width = pairs * HDIM
    slots = out.shape[0]
    rows = slots * 8
    stat_l = left[:, :, width:].reshape(rows, HDIM)
    stat_r = right[:, :, width:].reshape(rows, HDIM)
    peak = jnp.maximum(stat_l, stat_r)
    scale_l = jnp.exp2(stat_l - peak)
    scale_r = jnp.exp2(stat_r - peak)
    total = stat_l * pltpu.roll(scale_l, 64, 1) + stat_r * pltpu.roll(scale_r, 64, 1)
    column = lax.broadcasted_iota(jnp.int32, (rows, HDIM), 1)
    out[:, :, width:] = jnp.where(column < 64, peak, total).reshape(slots, 8, HDIM)
    for pair in range(pairs):
        at = pl.ds(pair * HDIM, HDIM)
        part_l = left[:, :, at].reshape(rows, HDIM) * scale_l[:, pair : pair + 1]
        part_r = right[:, :, at].reshape(rows, HDIM) * scale_r[:, pair : pair + 1]
        out[:, :, at] = (part_l + part_r).reshape(slots, 8, HDIM)


def kernel(n, sizes, q_ref, k_hbm, v_hbm, gain_ref, o_ref, *scratch):
    count = len(sizes)
    scratch = list(scratch)

    def take(many):
        taken = scratch[:many]
        del scratch[:many]
        return taken

    part, from_core, to_y, from_y, own, from_z = (take(count) for _ in range(6))
    k_buf, v_buf, packed, q_all, attended = take(5)
    kv_sem, gz_send, gz_recv, gy_send, gy_recv, gc_send, gc_recv = take(7)
    c_send, c_recv, y_send, y_recv, z_send, z_recv = take(6)

    nz = n // 4
    me = lax.axis_index("seq")
    z, y, core = me // 4, lax.rem(me // 2, 2), lax.rem(me, 2)
    sibling = z * 4 + y * 2 + (1 - core)
    across = z * 4 + (1 - y) * 2 + core
    offsets = list(range(1, nz))

    def z_peer(step):
        return lax.rem(z + step, nz)

    def device_at(zz):
        return zz * 4 + y * 2 + core

    starts = [sum(sizes[:i]) for i in range(count)]

    loads = []
    for i in range(count):
        columns = pl.ds(starts[i] * 4 * HDIM, sizes[i] * 4 * HDIM)
        pair = []
        for which, (hbm, buf) in enumerate(((k_hbm, k_buf), (v_hbm, v_buf))):
            copy = pltpu.make_async_copy(
                hbm.at[:, columns], buf.at[:, columns], kv_sem.at[i, which]
            )
            copy.start()
            pair.append(copy)
        loads.append(pair)

    barrier = pltpu.get_barrier_semaphore()
    for peer in [sibling, across] + [device_at(z_peer(s)) for s in offsets]:
        pl.semaphore_signal(
            barrier, inc=1, device_id={"seq": peer}, device_id_type=pl.DeviceIdType.MESH
        )

    quads = sum(sizes)
    mine = q_ref[...].astype(jnp.float32)
    for quad in range(quads):
        for j in range(4):
            head = quad * 4 + j
            packed[4 * j : 4 * j + 4, quad * HDIM : (quad + 1) * HDIM] = mine[
                :, head * HDIM : (head + 1) * HDIM
            ]
    base = core * (2 * nz) + y * nz
    other_base = core * (2 * nz) + (1 - y) * nz
    q_all[base + z] = packed[...].astype(jnp.bfloat16)

    pl.semaphore_wait(barrier, nz - 1 + 2)

    sends = []
    sib_base = (1 - core) * (2 * nz)

    def piece(i, first, slots=1):
        return q_all.at[pl.ds(first, slots), :, pl.ds(starts[i] * HDIM, sizes[i] * HDIM)]

    def send(*args):
        copy = remote(*args)
        copy.start()
        sends.append(copy)

    def gather_z(i):
        block = piece(i, base + z)
        for s in offsets:
            to = z_peer(s)
            send(block, block, gz_send.at[i, to], gz_recv.at[i, z], device_at(to))

    def gather_own(i):
        block = piece(i, base + z)
        send(block, block, gy_send.at[i, z], gy_recv.at[i, z], across)

    def gather_y(i):
        for s in offsets:
            src = z_peer(s)
            block = piece(i, base + src)
            remote(block, block, gz_send.at[i, src], gz_recv.at[i, src], device_at(src)).wait_recv()
            send(block, block, gy_send.at[i, src], gy_recv.at[i, src], across)
        near = piece(i, base, nz)
        send(near, near, gc_send.at[i, 0], gc_recv.at[i, 0], sibling)

    def gather_core(i):
        for s in [0] + offsets:
            src = z_peer(s)
            block = piece(i, other_base + src)
            remote(block, block, gy_send.at[i, src], gy_recv.at[i, src], across).wait_recv()
        far = piece(i, other_base, nz)
        send(far, far, gc_send.at[i, 1], gc_recv.at[i, 1], sibling)

    def gather_end(i):
        near = piece(i, sib_base + y * nz, nz)
        far = piece(i, sib_base + (1 - y) * nz, nz)
        remote(near, near, gc_send.at[i, 0], gc_recv.at[i, 0], sibling).wait_recv()
        remote(far, far, gc_send.at[i, 1], gc_recv.at[i, 1], sibling).wait_recv()

    gather_z(0)
    gather_own(0)
    for i in range(1, count):
        gather_z(i)
    gather_y(0)
    for i in range(1, count):
        gather_own(i)
    gather_core(0)

    rows = n * 8
    log_scale = math.log2(math.e) / math.sqrt(HDIM)
    first = lax.rem(lax.broadcasted_iota(jnp.int32, (rows, HDIM), 0), 8) < 4
    column = lax.broadcasted_iota(jnp.int32, (rows, HDIM), 1)

    def compute(i, middle):
        for copy in loads[i]:
            copy.wait()
        width = sizes[i] * 2 * HDIM
        out = part[i]

        def quad_step(step, stats):
            quad = starts[i] + step
            q_quad = q_all[:, :, pl.ds(quad * HDIM, HDIM)].astype(jnp.float32)
            for half in range(2):
                q_pair = q_quad[:, 8 * half : 8 * half + 8, :].reshape(rows, HDIM)
                spread = jnp.concatenate(
                    [jnp.where(first, q_pair, 0.0), jnp.where(first, 0.0, q_pair)], axis=1
                ).astype(jnp.bfloat16)
                at = pl.ds((quad * 2 + half) * 2 * HDIM, 2 * HDIM)
                scores = lax.dot_general(
                    spread, k_buf[:, at], (((1,), (1,)), ((), ())),
                    preferred_element_type=jnp.float32,
                )
                peak = jnp.max(scores, axis=1, keepdims=True) * log_scale
                weights = jnp.exp2(scores * log_scale - peak)
                total = jnp.sum(weights, axis=1, keepdims=True)
                high = weights.astype(jnp.bfloat16)
                low = (weights - high.astype(jnp.float32)).astype(jnp.bfloat16)
                both = jnp.dot(
                    jnp.concatenate([high, low], axis=0), v_buf[:, at],
                    preferred_element_type=jnp.float32,
                )
                summed = both[:rows] + both[rows:]
                picked = jnp.where(first, summed[:, :HDIM], summed[:, HDIM:])
                pair = step * 2 + half
                out[:, :, pl.ds(pair * HDIM, HDIM)] = picked.reshape(n, 8, HDIM)
                stats = jnp.where(column == pair, peak, stats)
                stats = jnp.where(column == pair + 64, total, stats)
            return stats

        stats = jnp.zeros((rows, HDIM), jnp.float32)
        for step in range(sizes[i]):
            stats = quad_step(step, stats)
            if step == 0:
                middle()
        out[:, :, width:] = stats.reshape(n, 8, HDIM)

    def start_core(i):
        copy = remote(
            part[i].at[pl.ds((1 - core) * (2 * nz), 2 * nz)], from_core[i],
            c_send.at[i], c_recv.at[i], sibling,
        )
        copy.start()
        return copy

    def start_y(i, core_copy):
        core_copy.wait_recv()
        pairs = sizes[i] * 2
        merge(
            part[i].at[pl.ds(other_base, nz)], from_core[i].at[pl.ds((1 - y) * nz, nz)], to_y[i], pairs
        )
        copy = remote(to_y[i], from_y[i], y_send.at[i], y_recv.at[i], across)
        copy.start()
        merge(part[i].at[pl.ds(base, nz)], from_core[i].at[pl.ds(y * nz, nz)], own[i], pairs)
        return copy

    to_z = part

    def start_z(i, y_copy, core_copy):
        y_copy.wait_recv()
        core_copy.wait_send()
        there = (1 - core) * (2 * nz)
        merge(own[i], from_y[i], to_z[i].at[pl.ds(there, nz)], sizes[i] * 2)
        copies = []
        for s in offsets:
            to = z_peer(s)
            copy = remote(
                to_z[i].at[there + to], from_z[i].at[z], z_send.at[i, to], z_recv.at[i, z], device_at(to)
            )
            copy.start()
            copies.append(copy)
        from_z[i][z] = to_z[i][there + z]
        return copies

    def finish(i):
        pairs = sizes[i] * 2
        width = pairs * HDIM
        for s in offsets:
            src = z_peer(s)
            remote(
                from_z[i].at[src], from_z[i].at[src], z_send.at[i, src], z_recv.at[i, src], device_at(src)
            ).wait_recv()
        stats = from_z[i][:, :, width:]
        peak = jnp.max(stats, axis=0)
        scales = [jnp.exp2(stats[k] - peak) for k in range(nz)]
        total = sum(stats[k] * pltpu.roll(scales[k], 64, 1) for k in range(nz))
        squares = jnp.zeros((8, HDIM), jnp.float32)
        for pair in range(pairs):
            at = pl.ds(pair * HDIM, HDIM)
            numer = sum(from_z[i][k, :, at] * scales[k][:, pair : pair + 1] for k in range(nz))
            value = numer / total[:, 64 + pair : 65 + pair]
            attended[:, pl.ds((starts[i] * 2 + pair) * HDIM, HDIM)] = value
            squares = squares + value * value
        return squares

    core_copies, y_copies, z_copies = [], [], []

    def advance(i):
        if i == 0:
            for later in range(1, count):
                gather_core(later)
        if i >= 1:
            y_copies.append(start_y(i - 1, core_copies[i - 1]))
        if i >= 2:
            z_copies.append(start_z(i - 2, y_copies[i - 2], core_copies[i - 2]))

    for i in range(count):
        gather_end(i)
        if i == 0:
            for later in range(1, count):
                gather_y(later)
        compute(i, functools.partial(advance, i))
        core_copies.append(start_core(i))
    squares = jnp.zeros((8, HDIM), jnp.float32)
    for i in range(count - 2):
        squares += finish(i)
    y_copies.append(start_y(count - 1, core_copies[-1]))
    for i in range(max(count - 2, 0), count):
        z_copies.append(start_z(i, y_copies[i], core_copies[i]))
    for i in range(max(count - 2, 0), count):
        squares += finish(i)
    squares = squares + pltpu.roll(squares, 4, 0)
    mean = jnp.sum(squares, axis=1, keepdims=True) * (1.0 / o_ref.shape[1])
    inverse = 1.0 / jnp.sqrt(mean + 1e-06)
    for pair in range(quads * 2):
        value = attended[:, pair * HDIM : (pair + 1) * HDIM] * inverse
        for j in range(2):
            at = pl.ds((pair * 2 + j) * HDIM, HDIM)
            o_ref[:, at] = (value[4 * j : 4 * j + 4] * gain_ref[:, at]).astype(jnp.bfloat16)

    for copy in sends + y_copies:
        copy.wait_send()
    for copies in z_copies:
        for copy in copies:
            copy.wait_send()


def shards(n, queries, keys, values, gain):
    rows_here, width = queries.shape
    tokens = keys.shape[0]
    quads = width // (4 * HDIM)
    sizes = chunk_sizes(quads)
    count = len(sizes)
    nz = n // 4
    wides = [(2 * size + 1) * HDIM for size in sizes]

    def per_chunk(slots):
        return [pltpu.VMEM((slots, 8, wide), jnp.float32) for wide in wides]

    dma = pltpu.SemaphoreType.DMA
    scratch = (
        per_chunk(n) + per_chunk(n // 2) + per_chunk(nz) + per_chunk(nz) + per_chunk(nz) + per_chunk(nz)
        + [
            pltpu.VMEM((tokens, width), jnp.bfloat16),
            pltpu.VMEM((tokens, width), jnp.bfloat16),
            pltpu.VMEM((16, quads * HDIM), jnp.float32),
            pltpu.VMEM((n, 16, quads * HDIM), jnp.bfloat16),
            pltpu.VMEM((8, quads * 2 * HDIM), jnp.float32),
        ]
        + [dma((count, 2))] + [dma((count, nz))] * 4 + [dma((count, 2))] * 2
        + [dma((count,)), dma((count,)), dma((count,)), dma((count,)), dma((count, nz)), dma((count, nz))]
    )
    vmem = pl.BlockSpec(memory_space=pltpu.VMEM)
    hbm = pl.BlockSpec(memory_space=pltpu.HBM)
    return pl.pallas_call(
        functools.partial(kernel, n, sizes),
        out_shape=jax.ShapeDtypeStruct((rows_here, width), jnp.bfloat16),
        in_specs=[vmem, hbm, hbm, vmem],
        out_specs=vmem,
        scratch_shapes=scratch,
        compiler_params=pltpu.CompilerParams(
            collective_id=0, has_side_effects=True, vmem_limit_bytes=56 * 1024 * 1024
        ),
    )(queries, keys, values, gain.reshape(1, width))


def solution(mesh):
    n = mesh.shape["seq"]
    in_specs = (P(("grp", "seq"), None), P(("grp", "seq"), None), P(("grp", "seq"), None), P())
    out_specs = P(("grp", "seq"), None)
    return jax.shard_map(
        functools.partial(shards, n), mesh=mesh, in_specs=in_specs, out_specs=out_specs, check_vma=False
    )
```

```python
import functools
import math

import jax
import jax.numpy as jnp
from jax import lax
from jax.experimental import pallas as pl
from jax.experimental.pallas import tpu as pltpu
from jax.sharding import PartitionSpec as P

HDIM = 128
CHUNK_QUADS = 2


def remote(src, dst, send_sem, recv_sem, peer):
    return pltpu.make_async_remote_copy(
        src_ref=src,
        dst_ref=dst,
        send_sem=send_sem,
        recv_sem=recv_sem,
        device_id={"seq": peer},
        device_id_type=pl.DeviceIdType.MESH,
    )


def merge(left, right, out, pairs):
    width = pairs * HDIM
    slots = out.shape[0]
    rows = slots * 8
    stat_l = left[:, :, width:].reshape(rows, HDIM)
    stat_r = right[:, :, width:].reshape(rows, HDIM)
    peak = jnp.maximum(stat_l, stat_r)
    scale_l = jnp.exp2(stat_l - peak)
    scale_r = jnp.exp2(stat_r - peak)
    total = stat_l * pltpu.roll(scale_l, 64, 1) + stat_r * pltpu.roll(scale_r, 64, 1)
    column = lax.broadcasted_iota(jnp.int32, (rows, HDIM), 1)
    out[:, :, width:] = jnp.where(column < 64, peak, total).reshape(slots, 8, HDIM)
    for pair in range(pairs):
        at = pl.ds(pair * HDIM, HDIM)
        part_l = left[:, :, at].reshape(rows, HDIM) * scale_l[:, pair : pair + 1]
        part_r = right[:, :, at].reshape(rows, HDIM) * scale_r[:, pair : pair + 1]
        out[:, :, at] = (part_l + part_r).reshape(slots, 8, HDIM)


def kernel(
    n, per, q_ref, k_hbm, v_hbm, gain_ref, o_ref,
    part, from_core, to_y, from_y, own, to_z, from_z, k_buf, v_buf, packed, q_all, attended,
    kv_sem, gz_send, gz_recv, gy_send, gy_recv, gc_send, gc_recv,
    c_send, c_recv, y_send, y_recv, z_send, z_recv,
):
    count = part.shape[0]
    quads = count * per
    pairs = per * 2
    width = pairs * HDIM
    nz = n // 4
    me = lax.axis_index("seq")
    z, y, core = me // 4, lax.rem(me // 2, 2), lax.rem(me, 2)
    sibling = z * 4 + y * 2 + (1 - core)
    across = z * 4 + (1 - y) * 2 + core
    offsets = list(range(1, nz))

    def z_peer(step):
        return lax.rem(z + step, nz)

    def device_at(zz):
        return zz * 4 + y * 2 + core

    def aligned(start, size):
        return pl.ds(pl.multiple_of(start, HDIM), size)

    def loads(c):
        columns = aligned(c * (per * 4 * HDIM), per * 4 * HDIM)
        return [
            pltpu.make_async_copy(hbm.at[:, columns], buf.at[:, columns], kv_sem.at[c, which])
            for which, (hbm, buf) in enumerate(((k_hbm, k_buf), (v_hbm, v_buf)))
        ]

    @pl.loop(0, count)
    def _(c):
        for copy in loads(c):
            copy.start()

    barrier = pltpu.get_barrier_semaphore()
    for peer in [sibling, across] + [device_at(z_peer(s)) for s in offsets]:
        pl.semaphore_signal(
            barrier, inc=1, device_id={"seq": peer}, device_id_type=pl.DeviceIdType.MESH
        )

    @pl.loop(0, quads)
    def _(quad):
        for j in range(4):
            block = q_ref[:, aligned((quad * 4 + j) * HDIM, HDIM)].astype(jnp.float32)
            packed[4 * j : 4 * j + 4, aligned(quad * HDIM, HDIM)] = block

    base = core * (2 * nz) + y * nz
    other_base = core * (2 * nz) + (1 - y) * nz
    q_all[base + z] = packed[...].astype(jnp.bfloat16)

    pl.semaphore_wait(barrier, nz - 1 + 2)

    own_block = q_all.at[base + z]
    sends = []
    for s in offsets:
        to = z_peer(s)
        copy = remote(own_block, own_block, gz_send.at[to], gz_recv.at[z], device_at(to))
        copy.start()
        sends.append(copy)
    copy = remote(own_block, own_block, gy_send.at[z], gy_recv.at[z], across)
    copy.start()
    sends.append(copy)
    for s in offsets:
        src = z_peer(s)
        block = q_all.at[base + src]
        remote(block, block, gz_send.at[src], gz_recv.at[src], device_at(src)).wait_recv()
        copy = remote(block, block, gy_send.at[src], gy_recv.at[src], across)
        copy.start()
        sends.append(copy)
    near = q_all.at[pl.ds(base, nz)]
    copy = remote(near, near, gc_send.at[0], gc_recv.at[0], sibling)
    copy.start()
    sends.append(copy)
    for s in [0] + offsets:
        src = z_peer(s)
        block = q_all.at[other_base + src]
        remote(block, block, gy_send.at[src], gy_recv.at[src], across).wait_recv()
    far = q_all.at[pl.ds(other_base, nz)]
    copy = remote(far, far, gc_send.at[1], gc_recv.at[1], sibling)
    copy.start()
    sends.append(copy)
    sib_base = (1 - core) * (2 * nz)
    sib_near = q_all.at[pl.ds(sib_base + y * nz, nz)]
    sib_far = q_all.at[pl.ds(sib_base + (1 - y) * nz, nz)]
    remote(sib_near, sib_near, gc_send.at[0], gc_recv.at[0], sibling).wait_recv()
    remote(sib_far, sib_far, gc_send.at[1], gc_recv.at[1], sibling).wait_recv()

    rows = n * 8
    log_scale = math.log2(math.e) / math.sqrt(HDIM)
    first = lax.rem(lax.broadcasted_iota(jnp.int32, (rows, HDIM), 0), 8) < 4
    column = lax.broadcasted_iota(jnp.int32, (rows, HDIM), 1)

    def compute(c):
        out = part.at[c]
        stats = jnp.zeros((rows, HDIM), jnp.float32)
        for step in range(per):
            quad = c * per + step
            q_quad = q_all[:, :, aligned(quad * HDIM, HDIM)].astype(jnp.float32)
            for half in range(2):
                q_pair = q_quad[:, 8 * half : 8 * half + 8, :].reshape(rows, HDIM)
                spread = jnp.concatenate(
                    [jnp.where(first, q_pair, 0.0), jnp.where(first, 0.0, q_pair)], axis=1
                ).astype(jnp.bfloat16)
                at = aligned((quad * 2 + half) * 2 * HDIM, 2 * HDIM)
                scores = lax.dot_general(
                    spread, k_buf[:, at], (((1,), (1,)), ((), ())),
                    preferred_element_type=jnp.float32,
                )
                peak = jnp.max(scores, axis=1, keepdims=True) * log_scale
                weights = jnp.exp2(scores * log_scale - peak)
                total = jnp.sum(weights, axis=1, keepdims=True)
                high = weights.astype(jnp.bfloat16)
                low = (weights - high.astype(jnp.float32)).astype(jnp.bfloat16)
                both = jnp.dot(
                    jnp.concatenate([high, low], axis=0), v_buf[:, at],
                    preferred_element_type=jnp.float32,
                )
                summed = both[:rows] + both[rows:]
                picked = jnp.where(first, summed[:, :HDIM], summed[:, HDIM:])
                pair = step * 2 + half
                out[:, :, pl.ds(pair * HDIM, HDIM)] = picked.reshape(n, 8, HDIM)
                stats = jnp.where(column == pair, peak, stats)
                stats = jnp.where(column == pair + 64, total, stats)
        out[:, :, width:] = stats.reshape(n, 8, HDIM)

    def core_copy(c):
        half = part.at[c, pl.ds((1 - core) * (2 * nz), 2 * nz)]
        return remote(half, from_core.at[c], c_send.at[c], c_recv.at[c], sibling)

    def y_copy(c):
        return remote(to_y.at[c], from_y.at[c], y_send.at[c], y_recv.at[c], across)

    def z_copy(c, s):
        to = z_peer(s)
        return remote(
            to_z.at[c, to], from_z.at[c, z], z_send.at[c, to], z_recv.at[c, z], device_at(to)
        )

    def z_arrival(c, s):
        src = z_peer(s)
        return remote(
            to_z.at[c, src], from_z.at[c, src], z_send.at[c, src], z_recv.at[c, src], device_at(src)
        )

    def start_y(c):
        core_copy(c).wait_recv()
        merge(
            part.at[c, pl.ds(other_base, nz)], from_core.at[c, pl.ds((1 - y) * nz, nz)], to_y.at[c], pairs
        )
        y_copy(c).start()
        merge(part.at[c, pl.ds(base, nz)], from_core.at[c, pl.ds(y * nz, nz)], own.at[c], pairs)

    def start_z(c):
        y_copy(c).wait_recv()
        merge(own.at[c], from_y.at[c], to_z.at[c], pairs)
        for s in offsets:
            z_copy(c, s).start()
        from_z[c, z] = to_z[c, z]

    def finish(c, squares):
        for s in offsets:
            z_arrival(c, s).wait_recv()
        stats = from_z[c, :, :, width:]
        peak = jnp.max(stats, axis=0)
        scales = [jnp.exp2(stats[k] - peak) for k in range(nz)]
        total = sum(stats[k] * pltpu.roll(scales[k], 64, 1) for k in range(nz))
        for pair in range(pairs):
            at = pl.ds(pair * HDIM, HDIM)
            numer = sum(from_z[c, k, :, at] * scales[k][:, pair : pair + 1] for k in range(nz))
            value = numer / total[:, 64 + pair : 65 + pair]
            attended[c, :, at] = value
            squares = squares + value * value
        return squares

    @pl.loop(0, count + 2)
    def _(c):
        @pl.when(c < count)
        def _():
            for copy in loads(c):
                copy.wait()
            compute(c)
            core_copy(c).start()

        @pl.when((c >= 1) & (c <= count))
        def _():
            start_y(c - 1)

        @pl.when(c >= 2)
        def _():
            start_z(c - 2)

    squares = lax.fori_loop(0, count, finish, jnp.zeros((8, HDIM), jnp.float32))
    squares = squares + pltpu.roll(squares, 4, 0)
    mean = jnp.sum(squares, axis=1, keepdims=True) * (1.0 / o_ref.shape[1])
    inverse = 1.0 / jnp.sqrt(mean + 1e-06)

    @pl.loop(0, count)
    def _(c):
        for pair in range(pairs):
            value = attended[c, :, pair * HDIM : (pair + 1) * HDIM] * inverse
            for j in range(2):
                at = aligned(((c * pairs + pair) * 2 + j) * HDIM, HDIM)
                o_ref[:, at] = (value[4 * j : 4 * j + 4] * gain_ref[:, at]).astype(jnp.bfloat16)
        core_copy(c).wait_send()
        y_copy(c).wait_send()
        for s in offsets:
            z_copy(c, s).wait_send()

    for copy in sends:
        copy.wait_send()


def shards(n, queries, keys, values, gain):
    rows_here, width = queries.shape
    tokens = keys.shape[0]
    quads = width // (4 * HDIM)
    per = CHUNK_QUADS if quads % CHUNK_QUADS == 0 else 1
    count = quads // per
    nz = n // 4
    wide = (2 * per + 1) * HDIM

    def per_chunk(slots):
        return pltpu.VMEM((count, slots, 8, wide), jnp.float32)

    dma = pltpu.SemaphoreType.DMA
    scratch = [per_chunk(n), per_chunk(n // 2)] + [per_chunk(nz)] * 5
    scratch += [
        pltpu.VMEM((tokens, width), jnp.bfloat16),
        pltpu.VMEM((tokens, width), jnp.bfloat16),
        pltpu.VMEM((16, quads * HDIM), jnp.float32),
        pltpu.VMEM((n, 16, quads * HDIM), jnp.bfloat16),
        pltpu.VMEM((count, 8, 2 * per * HDIM), jnp.float32),
    ]
    scratch += [dma((count, 2))] + [dma((nz,))] * 4 + [dma((2,))] * 2
    scratch += [dma((count,))] * 4 + [dma((count, nz))] * 2
    vmem = pl.BlockSpec(memory_space=pltpu.VMEM)
    hbm = pl.BlockSpec(memory_space=pltpu.HBM)
    return pl.pallas_call(
        functools.partial(kernel, n, per),
        out_shape=jax.ShapeDtypeStruct((rows_here, width), jnp.bfloat16),
        in_specs=[vmem, hbm, hbm, vmem],
        out_specs=vmem,
        scratch_shapes=scratch,
        compiler_params=pltpu.CompilerParams(
            collective_id=0, has_side_effects=True, vmem_limit_bytes=56 * 1024 * 1024
        ),
    )(queries, keys, values, gain.reshape(1, width))


def solution(mesh):
    n = mesh.shape["seq"]
    in_specs = (P(("grp", "seq"), None), P(("grp", "seq"), None), P(("grp", "seq"), None), P())
    out_specs = P(("grp", "seq"), None)
    return jax.shard_map(
        functools.partial(shards, n), mesh=mesh, in_specs=in_specs, out_specs=out_specs, check_vma=False
    )
```

```python
import functools
import math

import jax
import jax.numpy as jnp
from jax import lax
from jax.experimental import pallas as pl
from jax.experimental.pallas import tpu as pltpu
from jax.sharding import PartitionSpec as P

HDIM = 128
CHUNK_QUADS = 2


def remote(src, dst, send_sem, recv_sem, peer):
    return pltpu.make_async_remote_copy(
        src_ref=src,
        dst_ref=dst,
        send_sem=send_sem,
        recv_sem=recv_sem,
        device_id={"seq": peer},
        device_id_type=pl.DeviceIdType.MESH,
    )


def merge(left, right, out, pairs):
    width = pairs * HDIM
    slots = out.shape[0]
    rows = slots * 8
    stat_l = left[:, :, width:].reshape(rows, HDIM)
    stat_r = right[:, :, width:].reshape(rows, HDIM)
    peak = jnp.maximum(stat_l, stat_r)
    scale_l = jnp.exp2(stat_l - peak)
    scale_r = jnp.exp2(stat_r - peak)
    total = stat_l * pltpu.roll(scale_l, 64, 1) + stat_r * pltpu.roll(scale_r, 64, 1)
    column = lax.broadcasted_iota(jnp.int32, (rows, HDIM), 1)
    out[:, :, width:] = jnp.where(column < 64, peak, total).reshape(slots, 8, HDIM)
    for pair in range(pairs):
        at = pl.ds(pair * HDIM, HDIM)
        part_l = left[:, :, at].reshape(rows, HDIM) * scale_l[:, pair : pair + 1]
        part_r = right[:, :, at].reshape(rows, HDIM) * scale_r[:, pair : pair + 1]
        out[:, :, at] = (part_l + part_r).reshape(slots, 8, HDIM)


def kernel(
    n, per, q_ref, k_hbm, v_hbm, gain_ref, o_ref,
    part, from_core, to_y, from_y, own, to_z, from_z, k_buf, v_buf, packed, q_all, attended,
    kv_sem, gz_send, gz_recv, gy_send, gy_recv, gc_send, gc_recv,
    c_send, c_recv, y_send, y_recv, z_send, z_recv,
):
    count = part.shape[0]
    quads = count * per
    pairs = per * 2
    width = pairs * HDIM
    nz = n // 4
    me = lax.axis_index("seq")
    z, y, core = me // 4, lax.rem(me // 2, 2), lax.rem(me, 2)
    sibling = z * 4 + y * 2 + (1 - core)
    across = z * 4 + (1 - y) * 2 + core
    offsets = list(range(1, nz))

    def z_peer(step):
        return lax.rem(z + step, nz)

    def device_at(zz):
        return zz * 4 + y * 2 + core

    def aligned(start, size):
        return pl.ds(pl.multiple_of(start, HDIM), size)

    def loads(c):
        columns = aligned(c * (per * 4 * HDIM), per * 4 * HDIM)
        return [
            pltpu.make_async_copy(hbm.at[:, columns], buf.at[:, columns], kv_sem.at[c, which])
            for which, (hbm, buf) in enumerate(((k_hbm, k_buf), (v_hbm, v_buf)))
        ]

    @pl.loop(0, count)
    def _(c):
        for copy in loads(c):
            copy.start()

    barrier = pltpu.get_barrier_semaphore()
    for peer in [sibling, across] + [device_at(z_peer(s)) for s in offsets]:
        pl.semaphore_signal(
            barrier, inc=1, device_id={"seq": peer}, device_id_type=pl.DeviceIdType.MESH
        )

    @pl.loop(0, quads)
    def _(quad):
        for j in range(4):
            block = q_ref[:, aligned((quad * 4 + j) * HDIM, HDIM)].astype(jnp.float32)
            packed[4 * j : 4 * j + 4, aligned(quad * HDIM, HDIM)] = block

    base = core * (2 * nz) + y * nz
    other_base = core * (2 * nz) + (1 - y) * nz
    q_all[base + z] = packed[...].astype(jnp.bfloat16)

    pl.semaphore_wait(barrier, nz - 1 + 2)

    early = min(2, count - 1) * per
    sib_base = (1 - core) * (2 * nz)

    def piece(i, first, slots=1):
        columns = pl.ds(0, early * HDIM) if i == 0 else pl.ds(early * HDIM, (quads - early) * HDIM)
        return q_all.at[pl.ds(first, slots), :, columns]

    def gather_z(i, s):
        block, to = piece(i, base + z), z_peer(s)
        return remote(block, block, gz_send.at[i, to], gz_recv.at[i, z], device_at(to))

    def gather_z_arrival(i, s):
        src = z_peer(s)
        block = piece(i, base + src)
        return remote(block, block, gz_send.at[i, src], gz_recv.at[i, src], device_at(src))

    def gather_y(s):
        src = z_peer(s)
        block = piece(0, base + src)
        return remote(block, block, gy_send.at[src], gy_recv.at[src], across)

    def gather_y_arrival(s):
        src = z_peer(s)
        block = piece(0, other_base + src)
        return remote(block, block, gy_send.at[src], gy_recv.at[src], across)

    def gather_core(half):
        block = piece(0, base if half == 0 else other_base, nz)
        return remote(block, block, gc_send.at[half], gc_recv.at[half], sibling)

    def gather_core_arrival(half):
        block = piece(0, sib_base + (y if half == 0 else 1 - y) * nz, nz)
        return remote(block, block, gc_send.at[half], gc_recv.at[half], sibling)

    def late_y():
        block = piece(1, base, nz)
        return remote(block, block, gy_send.at[nz], gy_recv.at[nz], across)

    def late_y_arrival():
        block = piece(1, other_base, nz)
        return remote(block, block, gy_send.at[nz], gy_recv.at[nz], across)

    def late_core():
        block = piece(1, core * (2 * nz), 2 * nz)
        return remote(block, block, gc_send.at[2], gc_recv.at[2], sibling)

    def late_core_arrival():
        block = piece(1, sib_base, 2 * nz)
        return remote(block, block, gc_send.at[2], gc_recv.at[2], sibling)

    for s in offsets:
        gather_z(0, s).start()
    gather_y(0).start()
    for s in offsets:
        gather_z(1, s).start()
    for s in offsets:
        gather_z_arrival(0, s).wait_recv()
        gather_y(s).start()
    gather_core(0).start()
    for s in [0] + offsets:
        gather_y_arrival(s).wait_recv()
    gather_core(1).start()
    for s in offsets:
        gather_z_arrival(1, s).wait_recv()
    late_y().start()
    for half in range(2):
        gather_core_arrival(half).wait_recv()

    rows = n * 8
    log_scale = math.log2(math.e) / math.sqrt(HDIM)
    first = lax.rem(lax.broadcasted_iota(jnp.int32, (rows, HDIM), 0), 8) < 4
    column = lax.broadcasted_iota(jnp.int32, (rows, HDIM), 1)

    def compute(c, middle):
        out = part.at[c]
        stats = jnp.zeros((rows, HDIM), jnp.float32)
        for step in range(per):
            quad = c * per + step
            q_quad = q_all[:, :, aligned(quad * HDIM, HDIM)].astype(jnp.float32)
            for half in range(2):
                q_pair = q_quad[:, 8 * half : 8 * half + 8, :].reshape(rows, HDIM)
                spread = jnp.concatenate(
                    [jnp.where(first, q_pair, 0.0), jnp.where(first, 0.0, q_pair)], axis=1
                ).astype(jnp.bfloat16)
                at = aligned((quad * 2 + half) * 2 * HDIM, 2 * HDIM)
                scores = lax.dot_general(
                    spread, k_buf[:, at], (((1,), (1,)), ((), ())),
                    preferred_element_type=jnp.float32,
                )
                peak = jnp.max(scores, axis=1, keepdims=True) * log_scale
                weights = jnp.exp2(scores * log_scale - peak)
                total = jnp.sum(weights, axis=1, keepdims=True)
                high = weights.astype(jnp.bfloat16)
                low = (weights - high.astype(jnp.float32)).astype(jnp.bfloat16)
                both = jnp.dot(
                    jnp.concatenate([high, low], axis=0), v_buf[:, at],
                    preferred_element_type=jnp.float32,
                )
                summed = both[:rows] + both[rows:]
                picked = jnp.where(first, summed[:, :HDIM], summed[:, HDIM:])
                pair = step * 2 + half
                out[:, :, pl.ds(pair * HDIM, HDIM)] = picked.reshape(n, 8, HDIM)
                stats = jnp.where(column == pair, peak, stats)
                stats = jnp.where(column == pair + 64, total, stats)
            if step == 0:
                middle(c)
        out[:, :, width:] = stats.reshape(n, 8, HDIM)

    def core_copy(c):
        half = part.at[c, pl.ds((1 - core) * (2 * nz), 2 * nz)]
        return remote(half, from_core.at[c], c_send.at[c], c_recv.at[c], sibling)

    def y_copy(c):
        return remote(to_y.at[c], from_y.at[c], y_send.at[c], y_recv.at[c], across)

    def z_copy(c, s):
        to = z_peer(s)
        return remote(
            to_z.at[c, to], from_z.at[c, z], z_send.at[c, to], z_recv.at[c, z], device_at(to)
        )

    def z_arrival(c, s):
        src = z_peer(s)
        return remote(
            to_z.at[c, src], from_z.at[c, src], z_send.at[c, src], z_recv.at[c, src], device_at(src)
        )

    def start_y(c):
        core_copy(c).wait_recv()
        merge(
            part.at[c, pl.ds(other_base, nz)], from_core.at[c, pl.ds((1 - y) * nz, nz)], to_y.at[c], pairs
        )
        y_copy(c).start()
        merge(part.at[c, pl.ds(base, nz)], from_core.at[c, pl.ds(y * nz, nz)], own.at[c], pairs)

    def start_z(c):
        y_copy(c).wait_recv()
        merge(own.at[c], from_y.at[c], to_z.at[c], pairs)
        for s in offsets:
            z_copy(c, s).start()
        from_z[c, z] = to_z[c, z]

    def finish(c, squares):
        for s in offsets:
            z_arrival(c, s).wait_recv()
        stats = from_z[c, :, :, width:]
        peak = jnp.max(stats, axis=0)
        scales = [jnp.exp2(stats[k] - peak) for k in range(nz)]
        total = sum(stats[k] * pltpu.roll(scales[k], 64, 1) for k in range(nz))
        for pair in range(pairs):
            at = pl.ds(pair * HDIM, HDIM)
            numer = sum(from_z[c, k, :, at] * scales[k][:, pair : pair + 1] for k in range(nz))
            value = numer / total[:, 64 + pair : 65 + pair]
            attended[c, :, at] = value
            squares = squares + value * value
        return squares

    def advance(c):
        @pl.when(c >= 1)
        def _():
            start_y(c - 1)

        @pl.when(c >= 3)
        def _():
            start_z(c - 3)

        @pl.when(c == 1)
        def _():
            late_y_arrival().wait_recv()
            late_core().start()

    @pl.loop(0, count)
    def _(c):
        @pl.when(c == 2)
        def _():
            late_core_arrival().wait_recv()

        for copy in loads(c):
            copy.wait()
        compute(c, advance)
        core_copy(c).start()

    start_z(count - 3)
    start_y(count - 1)
    start_z(count - 2)
    squares = lax.fori_loop(0, count - 2, finish, jnp.zeros((8, HDIM), jnp.float32))
    start_z(count - 1)
    squares = lax.fori_loop(count - 2, count, finish, squares)
    squares = squares + pltpu.roll(squares, 4, 0)
    mean = jnp.sum(squares, axis=1, keepdims=True) * (1.0 / o_ref.shape[1])
    inverse = 1.0 / jnp.sqrt(mean + 1e-06)

    @pl.loop(0, count)
    def _(c):
        for pair in range(pairs):
            value = attended[c, :, pair * HDIM : (pair + 1) * HDIM] * inverse
            for j in range(2):
                at = aligned(((c * pairs + pair) * 2 + j) * HDIM, HDIM)
                o_ref[:, at] = (value[4 * j : 4 * j + 4] * gain_ref[:, at]).astype(jnp.bfloat16)
        core_copy(c).wait_send()
        y_copy(c).wait_send()
        for s in offsets:
            z_copy(c, s).wait_send()

    for s in offsets:
        gather_z(0, s).wait_send()
        gather_z(1, s).wait_send()
    for s in [0] + offsets:
        gather_y(s).wait_send()
    for copy in (gather_core(0), gather_core(1), late_y(), late_core()):
        copy.wait_send()


def shards(n, queries, keys, values, gain):
    rows_here, width = queries.shape
    tokens = keys.shape[0]
    quads = width // (4 * HDIM)
    per = CHUNK_QUADS if quads % CHUNK_QUADS == 0 else 1
    count = quads // per
    nz = n // 4
    wide = (2 * per + 1) * HDIM

    def per_chunk(slots):
        return pltpu.VMEM((count, slots, 8, wide), jnp.float32)

    dma = pltpu.SemaphoreType.DMA
    scratch = [per_chunk(n), per_chunk(n // 2)] + [per_chunk(nz)] * 5
    scratch += [
        pltpu.VMEM((tokens, width), jnp.bfloat16),
        pltpu.VMEM((tokens, width), jnp.bfloat16),
        pltpu.VMEM((16, quads * HDIM), jnp.float32),
        pltpu.VMEM((n, 16, quads * HDIM), jnp.bfloat16),
        pltpu.VMEM((count, 8, 2 * per * HDIM), jnp.float32),
    ]
    scratch += [dma((count, 2))] + [dma((2, nz))] * 2 + [dma((nz + 1,))] * 2 + [dma((3,))] * 2
    scratch += [dma((count,))] * 4 + [dma((count, nz))] * 2
    vmem = pl.BlockSpec(memory_space=pltpu.VMEM)
    hbm = pl.BlockSpec(memory_space=pltpu.HBM)
    return pl.pallas_call(
        functools.partial(kernel, n, per),
        out_shape=jax.ShapeDtypeStruct((rows_here, width), jnp.bfloat16),
        in_specs=[vmem, hbm, hbm, vmem],
        out_specs=vmem,
        scratch_shapes=scratch,
        compiler_params=pltpu.CompilerParams(
            collective_id=0, has_side_effects=True, vmem_limit_bytes=56 * 1024 * 1024
        ),
    )(queries, keys, values, gain.reshape(1, width))


def solution(mesh):
    n = mesh.shape["seq"]
    in_specs = (P(("grp", "seq"), None), P(("grp", "seq"), None), P(("grp", "seq"), None), P())
    out_specs = P(("grp", "seq"), None)
    return jax.shard_map(
        functools.partial(shards, n), mesh=mesh, in_specs=in_specs, out_specs=out_specs, check_vma=False
    )
```

```python
import functools
import math

import jax
import jax.numpy as jnp
from jax import lax
from jax.experimental import pallas as pl
from jax.experimental.pallas import tpu as pltpu
from jax.sharding import PartitionSpec as P

HDIM = 128
CHUNK_QUADS = 2


def remote(src, dst, send_sem, recv_sem, peer):
    return pltpu.make_async_remote_copy(
        src_ref=src,
        dst_ref=dst,
        send_sem=send_sem,
        recv_sem=recv_sem,
        device_id={"seq": peer},
        device_id_type=pl.DeviceIdType.MESH,
    )


def merge(left, right, out, pairs):
    width = pairs * HDIM
    slots = out.shape[0]
    rows = slots * 8
    stat_l = left[:, :, width:].reshape(rows, HDIM)
    stat_r = right[:, :, width:].reshape(rows, HDIM)
    peak = jnp.maximum(stat_l, stat_r)
    scale_l = jnp.exp2(stat_l - peak)
    scale_r = jnp.exp2(stat_r - peak)
    total = stat_l * pltpu.roll(scale_l, 64, 1) + stat_r * pltpu.roll(scale_r, 64, 1)
    column = lax.broadcasted_iota(jnp.int32, (rows, HDIM), 1)
    out[:, :, width:] = jnp.where(column < 64, peak, total).reshape(slots, 8, HDIM)
    for pair in range(pairs):
        at = pl.ds(pair * HDIM, HDIM)
        part_l = left[:, :, at].reshape(rows, HDIM) * scale_l[:, pair : pair + 1]
        part_r = right[:, :, at].reshape(rows, HDIM) * scale_r[:, pair : pair + 1]
        out[:, :, at] = (part_l + part_r).reshape(slots, 8, HDIM)


def kernel(
    n, per, q_ref, k_hbm, v_hbm, gain_ref, o_ref,
    part, from_core, to_y, from_y, own, to_z, from_z, k_buf, v_buf, packed, q_all, attended,
    kv_sem, gz_send, gz_recv, gy_send, gy_recv, gc_send, gc_recv,
    c_send, c_recv, y_send, y_recv, z_send, z_recv,
):
    count = part.shape[0]
    quads = count * per
    pairs = per * 2
    width = pairs * HDIM
    nz = n // 4
    me = lax.axis_index("seq")
    z, y, core = me // 4, lax.rem(me // 2, 2), lax.rem(me, 2)
    sibling = z * 4 + y * 2 + (1 - core)
    across = z * 4 + (1 - y) * 2 + core
    offsets = list(range(1, nz))

    def z_peer(step):
        return lax.rem(z + step, nz)

    def device_at(zz):
        return zz * 4 + y * 2 + core

    def aligned(start, size):
        return pl.ds(pl.multiple_of(start, HDIM), size)

    def loads(c):
        columns = aligned(c * (per * 4 * HDIM), per * 4 * HDIM)
        return [
            pltpu.make_async_copy(hbm.at[:, columns], buf.at[:, columns], kv_sem.at[c, which])
            for which, (hbm, buf) in enumerate(((k_hbm, k_buf), (v_hbm, v_buf)))
        ]

    @pl.loop(0, count)
    def _(c):
        for copy in loads(c):
            copy.start()

    barrier = pltpu.get_barrier_semaphore()
    for peer in [sibling, across] + [device_at(z_peer(s)) for s in offsets]:
        pl.semaphore_signal(
            barrier, inc=1, device_id={"seq": peer}, device_id_type=pl.DeviceIdType.MESH
        )

    @pl.loop(0, quads)
    def _(quad):
        for j in range(4):
            block = q_ref[:, aligned((quad * 4 + j) * HDIM, HDIM)].astype(jnp.float32)
            packed[4 * j : 4 * j + 4, aligned(quad * HDIM, HDIM)] = block

    base = core * (2 * nz) + y * nz
    other_base = core * (2 * nz) + (1 - y) * nz
    q_all[base + z] = packed[...].astype(jnp.bfloat16)

    pl.semaphore_wait(barrier, nz - 1 + 2)

    early = min(2, count - 1) * per
    sib_base = (1 - core) * (2 * nz)

    def piece(i, first, slots=1):
        columns = pl.ds(0, early * HDIM) if i == 0 else pl.ds(early * HDIM, (quads - early) * HDIM)
        return q_all.at[pl.ds(first, slots), :, columns]

    def gather_z(i, s):
        block, to = piece(i, base + z), z_peer(s)
        return remote(block, block, gz_send.at[i, to], gz_recv.at[i, z], device_at(to))

    def gather_z_arrival(i, s):
        src = z_peer(s)
        block = piece(i, base + src)
        return remote(block, block, gz_send.at[i, src], gz_recv.at[i, src], device_at(src))

    def gather_y(s):
        src = z_peer(s)
        block = piece(0, base + src)
        return remote(block, block, gy_send.at[src], gy_recv.at[src], across)

    def gather_y_arrival(s):
        src = z_peer(s)
        block = piece(0, other_base + src)
        return remote(block, block, gy_send.at[src], gy_recv.at[src], across)

    def gather_core(half):
        block = piece(0, base if half == 0 else other_base, nz)
        return remote(block, block, gc_send.at[half], gc_recv.at[half], sibling)

    def gather_core_arrival(half):
        block = piece(0, sib_base + (y if half == 0 else 1 - y) * nz, nz)
        return remote(block, block, gc_send.at[half], gc_recv.at[half], sibling)

    def late_y():
        block = piece(1, base, nz)
        return remote(block, block, gy_send.at[nz], gy_recv.at[nz], across)

    def late_y_arrival():
        block = piece(1, other_base, nz)
        return remote(block, block, gy_send.at[nz], gy_recv.at[nz], across)

    def late_core():
        block = piece(1, core * (2 * nz), 2 * nz)
        return remote(block, block, gc_send.at[2], gc_recv.at[2], sibling)

    def late_core_arrival():
        block = piece(1, sib_base, 2 * nz)
        return remote(block, block, gc_send.at[2], gc_recv.at[2], sibling)

    for s in offsets:
        gather_z(0, s).start()
    gather_y(0).start()
    for s in offsets:
        gather_z(1, s).start()
    for s in offsets:
        gather_z_arrival(0, s).wait_recv()
        gather_y(s).start()
    gather_core(0).start()
    for s in [0] + offsets:
        gather_y_arrival(s).wait_recv()
    gather_core(1).start()
    for s in offsets:
        gather_z_arrival(1, s).wait_recv()
    late_y().start()
    for half in range(2):
        gather_core_arrival(half).wait_recv()

    rows = n * 8
    log_scale = math.log2(math.e) / math.sqrt(HDIM)
    first = lax.rem(lax.broadcasted_iota(jnp.int32, (rows, HDIM), 0), 8) < 4
    first_lane = lax.rem(lax.broadcasted_iota(jnp.int32, (HDIM, rows), 1), 8) < 4
    line = lax.broadcasted_iota(jnp.int32, (HDIM, rows), 0)

    def compute(c, middle):
        out = part.at[c]
        stats = jnp.zeros((HDIM, rows), jnp.float32)
        for step in range(per):
            quad = c * per + step
            q_quad = q_all[:, :, aligned(quad * HDIM, HDIM)].astype(jnp.float32)
            for half in range(2):
                q_pair = q_quad[:, 8 * half : 8 * half + 8, :].reshape(rows, HDIM)
                turned = q_pair.T
                spread = jnp.concatenate(
                    [jnp.where(first_lane, turned, 0.0), jnp.where(first_lane, 0.0, turned)], axis=0
                ).astype(jnp.bfloat16)
                at = aligned((quad * 2 + half) * 2 * HDIM, 2 * HDIM)
                scores = jnp.dot(k_buf[:, at], spread, preferred_element_type=jnp.float32)
                peak = jnp.max(scores, axis=0, keepdims=True) * log_scale
                weights = jnp.exp2(scores * log_scale - peak)
                total = jnp.sum(weights, axis=0, keepdims=True)
                weights = weights.T
                high = weights.astype(jnp.bfloat16)
                low = (weights - high.astype(jnp.float32)).astype(jnp.bfloat16)
                both = jnp.dot(
                    jnp.concatenate([high, low], axis=0), v_buf[:, at],
                    preferred_element_type=jnp.float32,
                )
                summed = both[:rows] + both[rows:]
                picked = jnp.where(first, summed[:, :HDIM], summed[:, HDIM:])
                pair = step * 2 + half
                out[:, :, pl.ds(pair * HDIM, HDIM)] = picked.reshape(n, 8, HDIM)
                stats = jnp.where(line == pair, peak, stats)
                stats = jnp.where(line == pair + 64, total, stats)
            if step == 0:
                middle(c)
        out[:, :, width:] = stats.T.reshape(n, 8, HDIM)

    def core_copy(c):
        half = part.at[c, pl.ds((1 - core) * (2 * nz), 2 * nz)]
        return remote(half, from_core.at[c], c_send.at[c], c_recv.at[c], sibling)

    def y_copy(c):
        return remote(to_y.at[c], from_y.at[c], y_send.at[c], y_recv.at[c], across)

    def z_copy(c, s):
        to = z_peer(s)
        return remote(
            to_z.at[c, to], from_z.at[c, z], z_send.at[c, to], z_recv.at[c, z], device_at(to)
        )

    def z_arrival(c, s):
        src = z_peer(s)
        return remote(
            to_z.at[c, src], from_z.at[c, src], z_send.at[c, src], z_recv.at[c, src], device_at(src)
        )

    def start_y(c):
        core_copy(c).wait_recv()
        merge(
            part.at[c, pl.ds(other_base, nz)], from_core.at[c, pl.ds((1 - y) * nz, nz)], to_y.at[c], pairs
        )
        y_copy(c).start()
        merge(part.at[c, pl.ds(base, nz)], from_core.at[c, pl.ds(y * nz, nz)], own.at[c], pairs)

    def start_z(c):
        y_copy(c).wait_recv()
        merge(own.at[c], from_y.at[c], to_z.at[c], pairs)
        for s in offsets:
            z_copy(c, s).start()
        from_z[c, z] = to_z[c, z]

    def finish(c, squares):
        for s in offsets:
            z_arrival(c, s).wait_recv()
        stats = from_z[c, :, :, width:]
        peak = jnp.max(stats, axis=0)
        scales = [jnp.exp2(stats[k] - peak) for k in range(nz)]
        total = sum(stats[k] * pltpu.roll(scales[k], 64, 1) for k in range(nz))
        for pair in range(pairs):
            at = pl.ds(pair * HDIM, HDIM)
            numer = sum(from_z[c, k, :, at] * scales[k][:, pair : pair + 1] for k in range(nz))
            value = numer / total[:, 64 + pair : 65 + pair]
            attended[c, :, at] = value
            squares = squares + value * value
        return squares

    def advance(c):
        @pl.when(c >= 1)
        def _():
            start_y(c - 1)

        @pl.when(c >= 3)
        def _():
            start_z(c - 3)

        @pl.when(c == 1)
        def _():
            late_y_arrival().wait_recv()
            late_core().start()

    @pl.loop(0, count)
    def _(c):
        @pl.when(c == 2)
        def _():
            late_core_arrival().wait_recv()

        for copy in loads(c):
            copy.wait()
        compute(c, advance)
        core_copy(c).start()

    start_z(count - 3)
    start_y(count - 1)
    start_z(count - 2)
    squares = lax.fori_loop(0, count - 2, finish, jnp.zeros((8, HDIM), jnp.float32))
    start_z(count - 1)
    squares = lax.fori_loop(count - 2, count, finish, squares)
    squares = squares + pltpu.roll(squares, 4, 0)
    mean = jnp.sum(squares, axis=1, keepdims=True) * (1.0 / o_ref.shape[1])
    inverse = 1.0 / jnp.sqrt(mean + 1e-06)

    @pl.loop(0, count)
    def _(c):
        for pair in range(pairs):
            value = attended[c, :, pair * HDIM : (pair + 1) * HDIM] * inverse
            for j in range(2):
                at = aligned(((c * pairs + pair) * 2 + j) * HDIM, HDIM)
                o_ref[:, at] = (value[4 * j : 4 * j + 4] * gain_ref[:, at]).astype(jnp.bfloat16)
        core_copy(c).wait_send()
        y_copy(c).wait_send()
        for s in offsets:
            z_copy(c, s).wait_send()

    for s in offsets:
        gather_z(0, s).wait_send()
        gather_z(1, s).wait_send()
    for s in [0] + offsets:
        gather_y(s).wait_send()
    for copy in (gather_core(0), gather_core(1), late_y(), late_core()):
        copy.wait_send()


def shards(n, queries, keys, values, gain):
    rows_here, width = queries.shape
    tokens = keys.shape[0]
    quads = width // (4 * HDIM)
    per = CHUNK_QUADS if quads % CHUNK_QUADS == 0 else 1
    count = quads // per
    nz = n // 4
    wide = (2 * per + 1) * HDIM

    def per_chunk(slots):
        return pltpu.VMEM((count, slots, 8, wide), jnp.float32)

    dma = pltpu.SemaphoreType.DMA
    scratch = [per_chunk(n), per_chunk(n // 2)] + [per_chunk(nz)] * 5
    scratch += [
        pltpu.VMEM((tokens, width), jnp.bfloat16),
        pltpu.VMEM((tokens, width), jnp.bfloat16),
        pltpu.VMEM((16, quads * HDIM), jnp.float32),
        pltpu.VMEM((n, 16, quads * HDIM), jnp.bfloat16),
        pltpu.VMEM((count, 8, 2 * per * HDIM), jnp.float32),
    ]
    scratch += [dma((count, 2))] + [dma((2, nz))] * 2 + [dma((nz + 1,))] * 2 + [dma((3,))] * 2
    scratch += [dma((count,))] * 4 + [dma((count, nz))] * 2
    vmem = pl.BlockSpec(memory_space=pltpu.VMEM)
    hbm = pl.BlockSpec(memory_space=pltpu.HBM)
    return pl.pallas_call(
        functools.partial(kernel, n, per),
        out_shape=jax.ShapeDtypeStruct((rows_here, width), jnp.bfloat16),
        in_specs=[vmem, hbm, hbm, vmem],
        out_specs=vmem,
        scratch_shapes=scratch,
        compiler_params=pltpu.CompilerParams(
            collective_id=0, has_side_effects=True, vmem_limit_bytes=56 * 1024 * 1024
        ),
    )(queries, keys, values, gain.reshape(1, width))


def solution(mesh):
    n = mesh.shape["seq"]
    in_specs = (P(("grp", "seq"), None), P(("grp", "seq"), None), P(("grp", "seq"), None), P())
    out_specs = P(("grp", "seq"), None)
    return jax.shard_map(
        functools.partial(shards, n), mesh=mesh, in_specs=in_specs, out_specs=out_specs, check_vma=False
    )
```

```python
import functools
import math

import jax
import jax.numpy as jnp
from jax import lax
from jax.experimental import pallas as pl
from jax.experimental.pallas import tpu as pltpu
from jax.sharding import PartitionSpec as P

HDIM = 128
CHUNK_QUADS = 2


def remote(src, dst, send_sem, recv_sem, peer):
    return pltpu.make_async_remote_copy(
        src_ref=src,
        dst_ref=dst,
        send_sem=send_sem,
        recv_sem=recv_sem,
        device_id={"seq": peer},
        device_id_type=pl.DeviceIdType.MESH,
    )


def merge(left, right, out, pairs):
    width = pairs * HDIM
    slots = out.shape[0]
    rows = slots * 8
    stat_l = left[:, :, width:].reshape(rows, HDIM)
    stat_r = right[:, :, width:].reshape(rows, HDIM)
    peak = jnp.maximum(stat_l, stat_r)
    scale_l = jnp.exp2(stat_l - peak)
    scale_r = jnp.exp2(stat_r - peak)
    total = stat_l * pltpu.roll(scale_l, 64, 1) + stat_r * pltpu.roll(scale_r, 64, 1)
    column = lax.broadcasted_iota(jnp.int32, (rows, HDIM), 1)
    out[:, :, width:] = jnp.where(column < 64, peak, total).reshape(slots, 8, HDIM)
    for pair in range(pairs):
        at = pl.ds(pair * HDIM, HDIM)
        part_l = left[:, :, at].reshape(rows, HDIM) * scale_l[:, pair : pair + 1]
        part_r = right[:, :, at].reshape(rows, HDIM) * scale_r[:, pair : pair + 1]
        out[:, :, at] = (part_l + part_r).reshape(slots, 8, HDIM)


def kernel(
    n, per, q_ref, k_hbm, v_hbm, gain_ref, o_ref,
    part, from_core, to_y, from_y, own, to_z, from_z, k_buf, v_buf, packed, q_all, attended,
    kv_sem, gz_send, gz_recv, gy_send, gy_recv, gc_send, gc_recv,
    c_send, c_recv, y_send, y_recv, z_send, z_recv,
):
    count = part.shape[0]
    quads = count * per
    pairs = per * 2
    width = pairs * HDIM
    nz = n // 4
    me = lax.axis_index("seq")
    z, y, core = me // 4, lax.rem(me // 2, 2), lax.rem(me, 2)
    sibling = z * 4 + y * 2 + (1 - core)
    across = z * 4 + (1 - y) * 2 + core
    offsets = list(range(1, nz))

    def z_peer(step):
        return lax.rem(z + step, nz)

    def device_at(zz):
        return zz * 4 + y * 2 + core

    def aligned(start, size):
        return pl.ds(pl.multiple_of(start, HDIM), size)

    def loads(c):
        columns = aligned(c * (per * 4 * HDIM), per * 4 * HDIM)
        return [
            pltpu.make_async_copy(hbm.at[:, columns], buf.at[:, columns], kv_sem.at[c, which])
            for which, (hbm, buf) in enumerate(((k_hbm, k_buf), (v_hbm, v_buf)))
        ]

    @pl.loop(0, count)
    def _(c):
        for copy in loads(c):
            copy.start()

    barrier = pltpu.get_barrier_semaphore()
    for peer in [sibling, across] + [device_at(z_peer(s)) for s in offsets]:
        pl.semaphore_signal(
            barrier, inc=1, device_id={"seq": peer}, device_id_type=pl.DeviceIdType.MESH
        )

    @pl.loop(0, quads)
    def _(quad):
        for j in range(4):
            block = q_ref[:, aligned((quad * 4 + j) * HDIM, HDIM)].astype(jnp.float32)
            packed[4 * j : 4 * j + 4, aligned(quad * HDIM, HDIM)] = block

    base = core * (2 * nz) + y * nz
    other_base = core * (2 * nz) + (1 - y) * nz
    q_all[base + z] = packed[...].astype(jnp.bfloat16)

    pl.semaphore_wait(barrier, nz - 1 + 2)

    early = min(2, count - 1) * per
    sib_base = (1 - core) * (2 * nz)

    def piece(i, first, slots=1):
        columns = pl.ds(0, early * HDIM) if i == 0 else pl.ds(early * HDIM, (quads - early) * HDIM)
        return q_all.at[pl.ds(first, slots), :, columns]

    def gather_z(i, s):
        block, to = piece(i, base + z), z_peer(s)
        return remote(block, block, gz_send.at[i, to], gz_recv.at[i, z], device_at(to))

    def gather_z_arrival(i, s):
        src = z_peer(s)
        block = piece(i, base + src)
        return remote(block, block, gz_send.at[i, src], gz_recv.at[i, src], device_at(src))

    def gather_y(s):
        src = z_peer(s)
        block = piece(0, base + src)
        return remote(block, block, gy_send.at[src], gy_recv.at[src], across)

    def gather_y_arrival(s):
        src = z_peer(s)
        block = piece(0, other_base + src)
        return remote(block, block, gy_send.at[src], gy_recv.at[src], across)

    def gather_core(half):
        block = piece(0, base if half == 0 else other_base, nz)
        return remote(block, block, gc_send.at[half], gc_recv.at[half], sibling)

    def gather_core_arrival(half):
        block = piece(0, sib_base + (y if half == 0 else 1 - y) * nz, nz)
        return remote(block, block, gc_send.at[half], gc_recv.at[half], sibling)

    def late_y():
        block = piece(1, base, nz)
        return remote(block, block, gy_send.at[nz], gy_recv.at[nz], across)

    def late_y_arrival():
        block = piece(1, other_base, nz)
        return remote(block, block, gy_send.at[nz], gy_recv.at[nz], across)

    def late_core():
        block = piece(1, core * (2 * nz), 2 * nz)
        return remote(block, block, gc_send.at[2], gc_recv.at[2], sibling)

    def late_core_arrival():
        block = piece(1, sib_base, 2 * nz)
        return remote(block, block, gc_send.at[2], gc_recv.at[2], sibling)

    for s in offsets:
        gather_z(0, s).start()
    gather_y(0).start()
    for s in offsets:
        gather_z(1, s).start()
    for s in offsets:
        gather_z_arrival(0, s).wait_recv()
        gather_y(s).start()
    gather_core(0).start()
    for s in [0] + offsets:
        gather_y_arrival(s).wait_recv()
    gather_core(1).start()
    for s in offsets:
        gather_z_arrival(1, s).wait_recv()
    late_y().start()
    for half in range(2):
        gather_core_arrival(half).wait_recv()

    rows = n * 8
    log_scale = math.log2(math.e) / math.sqrt(HDIM)
    first = lax.rem(lax.broadcasted_iota(jnp.int32, (rows, HDIM), 0), 8) < 4
    column = lax.broadcasted_iota(jnp.int32, (rows, HDIM), 1)

    def pair_columns(c, pair):
        return aligned((c * pairs + pair) * 2 * HDIM, 2 * HDIM)

    def compute(c, middle):
        out = part.at[c]
        stats = jnp.zeros((rows, HDIM), jnp.float32)
        scores = []
        for pair in range(pairs):
            quad = c * per + pair // 2
            q_quad = q_all[:, :, aligned(quad * HDIM, HDIM)].astype(jnp.float32)
            half = pair % 2
            q_pair = q_quad[:, 8 * half : 8 * half + 8, :].reshape(rows, HDIM)
            spread = jnp.concatenate(
                [jnp.where(first, q_pair, 0.0), jnp.where(first, 0.0, q_pair)], axis=1
            ).astype(jnp.bfloat16)
            scores.append(
                lax.dot_general(
                    spread, k_buf[:, pair_columns(c, pair)], (((1,), (1,)), ((), ())),
                    preferred_element_type=jnp.float32,
                )
            )
        middle(c)
        peaks = [jnp.max(score, axis=1, keepdims=True) * log_scale for score in scores]
        weights = [jnp.exp2(score * log_scale - peak) for score, peak in zip(scores, peaks)]
        split = []
        for weight in weights:
            high = weight.astype(jnp.bfloat16)
            low = (weight - high.astype(jnp.float32)).astype(jnp.bfloat16)
            split.append(jnp.concatenate([high, low], axis=0))
        products = [
            jnp.dot(split[pair], v_buf[:, pair_columns(c, pair)], preferred_element_type=jnp.float32)
            for pair in range(pairs)
        ]
        totals = [jnp.sum(weight, axis=1, keepdims=True) for weight in weights]
        for pair in range(pairs):
            summed = products[pair][:rows] + products[pair][rows:]
            picked = jnp.where(first, summed[:, :HDIM], summed[:, HDIM:])
            out[:, :, pl.ds(pair * HDIM, HDIM)] = picked.reshape(n, 8, HDIM)
            stats = jnp.where(column == pair, peaks[pair], stats)
            stats = jnp.where(column == pair + 64, totals[pair], stats)
        out[:, :, width:] = stats.reshape(n, 8, HDIM)

    def core_copy(c):
        half = part.at[c, pl.ds((1 - core) * (2 * nz), 2 * nz)]
        return remote(half, from_core.at[c], c_send.at[c], c_recv.at[c], sibling)

    def y_copy(c):
        return remote(to_y.at[c], from_y.at[c], y_send.at[c], y_recv.at[c], across)

    def z_copy(c, s):
        to = z_peer(s)
        return remote(
            to_z.at[c, to], from_z.at[c, z], z_send.at[c, to], z_recv.at[c, z], device_at(to)
        )

    def z_arrival(c, s):
        src = z_peer(s)
        return remote(
            to_z.at[c, src], from_z.at[c, src], z_send.at[c, src], z_recv.at[c, src], device_at(src)
        )

    def start_y(c):
        core_copy(c).wait_recv()
        merge(
            part.at[c, pl.ds(other_base, nz)], from_core.at[c, pl.ds((1 - y) * nz, nz)], to_y.at[c], pairs
        )
        y_copy(c).start()
        merge(part.at[c, pl.ds(base, nz)], from_core.at[c, pl.ds(y * nz, nz)], own.at[c], pairs)

    def start_z(c):
        y_copy(c).wait_recv()
        merge(own.at[c], from_y.at[c], to_z.at[c], pairs)
        for s in offsets:
            z_copy(c, s).start()
        from_z[c, z] = to_z[c, z]

    def finish(c, squares):
        for s in offsets:
            z_arrival(c, s).wait_recv()
        stats = from_z[c, :, :, width:]
        peak = jnp.max(stats, axis=0)
        scales = [jnp.exp2(stats[k] - peak) for k in range(nz)]
        total = sum(stats[k] * pltpu.roll(scales[k], 64, 1) for k in range(nz))
        for pair in range(pairs):
            at = pl.ds(pair * HDIM, HDIM)
            numer = sum(from_z[c, k, :, at] * scales[k][:, pair : pair + 1] for k in range(nz))
            value = numer / total[:, 64 + pair : 65 + pair]
            attended[c, :, at] = value
            squares = squares + value * value
        return squares

    def advance(c):
        @pl.when(c >= 1)
        def _():
            start_y(c - 1)

        @pl.when(c >= 3)
        def _():
            start_z(c - 3)

        @pl.when(c == 1)
        def _():
            late_y_arrival().wait_recv()
            late_core().start()

    @pl.loop(0, count)
    def _(c):
        @pl.when(c == 2)
        def _():
            late_core_arrival().wait_recv()

        for copy in loads(c):
            copy.wait()
        compute(c, advance)
        core_copy(c).start()

    start_z(count - 3)
    start_y(count - 1)
    start_z(count - 2)
    squares = lax.fori_loop(0, count - 2, finish, jnp.zeros((8, HDIM), jnp.float32))
    start_z(count - 1)
    squares = lax.fori_loop(count - 2, count, finish, squares)
    squares = squares + pltpu.roll(squares, 4, 0)
    mean = jnp.sum(squares, axis=1, keepdims=True) * (1.0 / o_ref.shape[1])
    inverse = 1.0 / jnp.sqrt(mean + 1e-06)

    @pl.loop(0, count)
    def _(c):
        for pair in range(pairs):
            value = attended[c, :, pair * HDIM : (pair + 1) * HDIM] * inverse
            for j in range(2):
                at = aligned(((c * pairs + pair) * 2 + j) * HDIM, HDIM)
                o_ref[:, at] = (value[4 * j : 4 * j + 4] * gain_ref[:, at]).astype(jnp.bfloat16)
        core_copy(c).wait_send()
        y_copy(c).wait_send()
        for s in offsets:
            z_copy(c, s).wait_send()

    for s in offsets:
        gather_z(0, s).wait_send()
        gather_z(1, s).wait_send()
    for s in [0] + offsets:
        gather_y(s).wait_send()
    for copy in (gather_core(0), gather_core(1), late_y(), late_core()):
        copy.wait_send()


def shards(n, queries, keys, values, gain):
    rows_here, width = queries.shape
    tokens = keys.shape[0]
    quads = width // (4 * HDIM)
    per = CHUNK_QUADS if quads % CHUNK_QUADS == 0 else 1
    count = quads // per
    nz = n // 4
    wide = (2 * per + 1) * HDIM

    def per_chunk(slots):
        return pltpu.VMEM((count, slots, 8, wide), jnp.float32)

    dma = pltpu.SemaphoreType.DMA
    scratch = [per_chunk(n), per_chunk(n // 2)] + [per_chunk(nz)] * 5
    scratch += [
        pltpu.VMEM((tokens, width), jnp.bfloat16),
        pltpu.VMEM((tokens, width), jnp.bfloat16),
        pltpu.VMEM((16, quads * HDIM), jnp.float32),
        pltpu.VMEM((n, 16, quads * HDIM), jnp.bfloat16),
        pltpu.VMEM((count, 8, 2 * per * HDIM), jnp.float32),
    ]
    scratch += [dma((count, 2))] + [dma((2, nz))] * 2 + [dma((nz + 1,))] * 2 + [dma((3,))] * 2
    scratch += [dma((count,))] * 4 + [dma((count, nz))] * 2
    vmem = pl.BlockSpec(memory_space=pltpu.VMEM)
    hbm = pl.BlockSpec(memory_space=pltpu.HBM)
    return pl.pallas_call(
        functools.partial(kernel, n, per),
        out_shape=jax.ShapeDtypeStruct((rows_here, width), jnp.bfloat16),
        in_specs=[vmem, hbm, hbm, vmem],
        out_specs=vmem,
        scratch_shapes=scratch,
        compiler_params=pltpu.CompilerParams(
            collective_id=0, has_side_effects=True, vmem_limit_bytes=56 * 1024 * 1024
        ),
    )(queries, keys, values, gain.reshape(1, width))


def solution(mesh):
    n = mesh.shape["seq"]
    in_specs = (P(("grp", "seq"), None), P(("grp", "seq"), None), P(("grp", "seq"), None), P())
    out_specs = P(("grp", "seq"), None)
    return jax.shard_map(
        functools.partial(shards, n), mesh=mesh, in_specs=in_specs, out_specs=out_specs, check_vma=False
    )
```

```python
import functools
import math

import jax
import jax.numpy as jnp
from jax import lax
from jax.experimental import pallas as pl
from jax.experimental.pallas import tpu as pltpu
from jax.sharding import PartitionSpec as P

HDIM = 128
CHUNK_QUADS = 2


def remote(src, dst, send_sem, recv_sem, peer):
    return pltpu.make_async_remote_copy(
        src_ref=src,
        dst_ref=dst,
        send_sem=send_sem,
        recv_sem=recv_sem,
        device_id={"seq": peer},
        device_id_type=pl.DeviceIdType.MESH,
    )


def merge(left, right, out, pairs):
    width = pairs * HDIM
    slots = out.shape[0]
    rows = slots * 8
    stat_l = left[:, :, width:].reshape(rows, HDIM)
    stat_r = right[:, :, width:].reshape(rows, HDIM)
    peak = jnp.maximum(stat_l, stat_r)
    scale_l = jnp.exp2(stat_l - peak)
    scale_r = jnp.exp2(stat_r - peak)
    total = stat_l * pltpu.roll(scale_l, 64, 1) + stat_r * pltpu.roll(scale_r, 64, 1)
    column = lax.broadcasted_iota(jnp.int32, (rows, HDIM), 1)
    out[:, :, width:] = jnp.where(column < 64, peak, total).reshape(slots, 8, HDIM)
    for pair in range(pairs):
        at = pl.ds(pair * HDIM, HDIM)
        part_l = left[:, :, at].reshape(rows, HDIM) * scale_l[:, pair : pair + 1]
        part_r = right[:, :, at].reshape(rows, HDIM) * scale_r[:, pair : pair + 1]
        out[:, :, at] = (part_l + part_r).reshape(slots, 8, HDIM)


def kernel(
    n, per, q_ref, k_hbm, v_hbm, gain_ref, o_ref,
    part, from_core, to_y, from_y, own, to_z, from_z, k_buf, v_buf, packed, q_all, attended, score_buf,
    kv_sem, gz_send, gz_recv, gy_send, gy_recv, gc_send, gc_recv,
    c_send, c_recv, y_send, y_recv, z_send, z_recv,
):
    count = part.shape[0]
    quads = count * per
    pairs = per * 2
    width = pairs * HDIM
    nz = n // 4
    me = lax.axis_index("seq")
    z, y, core = me // 4, lax.rem(me // 2, 2), lax.rem(me, 2)
    sibling = z * 4 + y * 2 + (1 - core)
    across = z * 4 + (1 - y) * 2 + core
    offsets = list(range(1, nz))

    def z_peer(step):
        return lax.rem(z + step, nz)

    def device_at(zz):
        return zz * 4 + y * 2 + core

    def aligned(start, size):
        return pl.ds(pl.multiple_of(start, HDIM), size)

    def load(c, which):
        columns = aligned(c * (per * 4 * HDIM), per * 4 * HDIM)
        hbm, buf = ((k_hbm, k_buf), (v_hbm, v_buf))[which]
        return pltpu.make_async_copy(hbm.at[:, columns], buf.at[:, columns], kv_sem.at[c, which])

    @pl.loop(0, count)
    def _(c):
        load(c, 0).start()
        load(c, 1).start()

    barrier = pltpu.get_barrier_semaphore()
    for peer in [sibling, across] + [device_at(z_peer(s)) for s in offsets]:
        pl.semaphore_signal(
            barrier, inc=1, device_id={"seq": peer}, device_id_type=pl.DeviceIdType.MESH
        )

    @pl.loop(0, quads)
    def _(quad):
        for j in range(4):
            block = q_ref[:, aligned((quad * 4 + j) * HDIM, HDIM)].astype(jnp.float32)
            packed[4 * j : 4 * j + 4, aligned(quad * HDIM, HDIM)] = block

    base = core * (2 * nz) + y * nz
    other_base = core * (2 * nz) + (1 - y) * nz
    q_all[base + z] = packed[...].astype(jnp.bfloat16)

    pl.semaphore_wait(barrier, nz - 1 + 2)

    early = min(3, count - 1) * per
    sib_base = (1 - core) * (2 * nz)

    def piece(i, first, slots=1):
        columns = pl.ds(0, early * HDIM) if i == 0 else pl.ds(early * HDIM, (quads - early) * HDIM)
        return q_all.at[pl.ds(first, slots), :, columns]

    def gather_z(i, s):
        block, to = piece(i, base + z), z_peer(s)
        return remote(block, block, gz_send.at[i, to], gz_recv.at[i, z], device_at(to))

    def gather_z_arrival(i, s):
        src = z_peer(s)
        block = piece(i, base + src)
        return remote(block, block, gz_send.at[i, src], gz_recv.at[i, src], device_at(src))

    def gather_y(s):
        src = z_peer(s)
        block = piece(0, base + src)
        return remote(block, block, gy_send.at[src], gy_recv.at[src], across)

    def gather_y_arrival(s):
        src = z_peer(s)
        block = piece(0, other_base + src)
        return remote(block, block, gy_send.at[src], gy_recv.at[src], across)

    def gather_core(half):
        block = piece(0, base if half == 0 else other_base, nz)
        return remote(block, block, gc_send.at[half], gc_recv.at[half], sibling)

    def gather_core_arrival(half):
        block = piece(0, sib_base + (y if half == 0 else 1 - y) * nz, nz)
        return remote(block, block, gc_send.at[half], gc_recv.at[half], sibling)

    def late_y():
        block = piece(1, base, nz)
        return remote(block, block, gy_send.at[nz], gy_recv.at[nz], across)

    def late_y_arrival():
        block = piece(1, other_base, nz)
        return remote(block, block, gy_send.at[nz], gy_recv.at[nz], across)

    def late_core():
        block = piece(1, core * (2 * nz), 2 * nz)
        return remote(block, block, gc_send.at[2], gc_recv.at[2], sibling)

    def late_core_arrival():
        block = piece(1, sib_base, 2 * nz)
        return remote(block, block, gc_send.at[2], gc_recv.at[2], sibling)

    for s in offsets:
        gather_z(0, s).start()
    gather_y(0).start()
    for s in offsets:
        gather_z(1, s).start()
    for s in offsets:
        gather_z_arrival(0, s).wait_recv()
        gather_y(s).start()
    gather_core(0).start()
    for s in [0] + offsets:
        gather_y_arrival(s).wait_recv()
    gather_core(1).start()
    for s in offsets:
        gather_z_arrival(1, s).wait_recv()
    late_y().start()
    for half in range(2):
        gather_core_arrival(half).wait_recv()

    rows = n * 8
    log_scale = math.log2(math.e) / math.sqrt(HDIM)
    first = lax.rem(lax.broadcasted_iota(jnp.int32, (rows, HDIM), 0), 8) < 4
    column = lax.broadcasted_iota(jnp.int32, (rows, HDIM), 1)

    def pair_columns(c, pair):
        return aligned((c * pairs + pair) * 2 * HDIM, 2 * HDIM)

    def score(c, pair):
        quad = c * per + pair // 2
        q_quad = q_all[:, :, aligned(quad * HDIM, HDIM)].astype(jnp.float32)
        half = pair % 2
        q_pair = q_quad[:, 8 * half : 8 * half + 8, :].reshape(rows, HDIM)
        spread = jnp.concatenate(
            [jnp.where(first, q_pair, 0.0), jnp.where(first, 0.0, q_pair)], axis=1
        ).astype(jnp.bfloat16)
        score_buf[pair] = lax.dot_general(
            spread, k_buf[:, pair_columns(c, pair)], (((1,), (1,)), ((), ())),
            preferred_element_type=jnp.float32,
        )

    def compute(c, following, middle):
        out = part.at[c]
        stats = jnp.zeros((rows, HDIM), jnp.float32)
        peaks, totals, split = [], [], []
        for pair in range(pairs):
            peak = jnp.max(score_buf[pair], axis=1, keepdims=True) * log_scale
            weight = jnp.exp2(score_buf[pair] * log_scale - peak)
            high = weight.astype(jnp.bfloat16)
            low = (weight - high.astype(jnp.float32)).astype(jnp.bfloat16)
            split.append(jnp.concatenate([high, low], axis=0))
            peaks.append(peak)
            totals.append(jnp.sum(weight, axis=1, keepdims=True))
            if following:
                score(c + 1, pair)
        middle(c)
        products = [
            jnp.dot(split[pair], v_buf[:, pair_columns(c, pair)], preferred_element_type=jnp.float32)
            for pair in range(pairs)
        ]
        for pair in range(pairs):
            summed = products[pair][:rows] + products[pair][rows:]
            picked = jnp.where(first, summed[:, :HDIM], summed[:, HDIM:])
            out[:, :, pl.ds(pair * HDIM, HDIM)] = picked.reshape(n, 8, HDIM)
            stats = jnp.where(column == pair, peaks[pair], stats)
            stats = jnp.where(column == pair + 64, totals[pair], stats)
        out[:, :, width:] = stats.reshape(n, 8, HDIM)

    def core_copy(c):
        half = part.at[c, pl.ds((1 - core) * (2 * nz), 2 * nz)]
        return remote(half, from_core.at[c], c_send.at[c], c_recv.at[c], sibling)

    def y_copy(c):
        return remote(to_y.at[c], from_y.at[c], y_send.at[c], y_recv.at[c], across)

    def z_copy(c, s):
        to = z_peer(s)
        return remote(
            to_z.at[c, to], from_z.at[c, z], z_send.at[c, to], z_recv.at[c, z], device_at(to)
        )

    def z_arrival(c, s):
        src = z_peer(s)
        return remote(
            to_z.at[c, src], from_z.at[c, src], z_send.at[c, src], z_recv.at[c, src], device_at(src)
        )

    def start_y(c):
        core_copy(c).wait_recv()
        merge(
            part.at[c, pl.ds(other_base, nz)], from_core.at[c, pl.ds((1 - y) * nz, nz)], to_y.at[c], pairs
        )
        y_copy(c).start()
        merge(part.at[c, pl.ds(base, nz)], from_core.at[c, pl.ds(y * nz, nz)], own.at[c], pairs)

    def start_z(c):
        y_copy(c).wait_recv()
        merge(own.at[c], from_y.at[c], to_z.at[c], pairs)
        for s in offsets:
            z_copy(c, s).start()
        from_z[c, z] = to_z[c, z]

    def finish(c, squares):
        for s in offsets:
            z_arrival(c, s).wait_recv()
        stats = from_z[c, :, :, width:]
        peak = jnp.max(stats, axis=0)
        scales = [jnp.exp2(stats[k] - peak) for k in range(nz)]
        total = sum(stats[k] * pltpu.roll(scales[k], 64, 1) for k in range(nz))
        for pair in range(pairs):
            at = pl.ds(pair * HDIM, HDIM)
            numer = sum(from_z[c, k, :, at] * scales[k][:, pair : pair + 1] for k in range(nz))
            value = numer / total[:, 64 + pair : 65 + pair]
            attended[c, :, at] = value
            squares = squares + value * value
        return squares

    def advance(c):
        @pl.when(c >= 1)
        def _():
            start_y(c - 1)

        @pl.when(c >= 3)
        def _():
            start_z(c - 3)

        @pl.when(c == 1)
        def _():
            late_y_arrival().wait_recv()
            late_core().start()

    load(0, 0).wait()
    for pair in range(pairs):
        score(0, pair)

    @pl.loop(0, count - 1)
    def _(c):
        @pl.when(c == 2)
        def _():
            late_core_arrival().wait_recv()

        load(c + 1, 0).wait()
        load(c, 1).wait()
        compute(c, True, advance)
        core_copy(c).start()

    last = count - 1
    load(last, 1).wait()
    compute(last, False, advance)
    core_copy(last).start()

    start_z(count - 3)
    start_y(count - 1)
    start_z(count - 2)
    squares = lax.fori_loop(0, count - 2, finish, jnp.zeros((8, HDIM), jnp.float32))
    start_z(count - 1)
    squares = lax.fori_loop(count - 2, count, finish, squares)
    squares = squares + pltpu.roll(squares, 4, 0)
    mean = jnp.sum(squares, axis=1, keepdims=True) * (1.0 / o_ref.shape[1])
    inverse = 1.0 / jnp.sqrt(mean + 1e-06)

    @pl.loop(0, count)
    def _(c):
        for pair in range(pairs):
            value = attended[c, :, pair * HDIM : (pair + 1) * HDIM] * inverse
            for j in range(2):
                at = aligned(((c * pairs + pair) * 2 + j) * HDIM, HDIM)
                o_ref[:, at] = (value[4 * j : 4 * j + 4] * gain_ref[:, at]).astype(jnp.bfloat16)
        core_copy(c).wait_send()
        y_copy(c).wait_send()
        for s in offsets:
            z_copy(c, s).wait_send()

    for s in offsets:
        gather_z(0, s).wait_send()
        gather_z(1, s).wait_send()
    for s in [0] + offsets:
        gather_y(s).wait_send()
    for copy in (gather_core(0), gather_core(1), late_y(), late_core()):
        copy.wait_send()


def shards(n, queries, keys, values, gain):
    rows_here, width = queries.shape
    tokens = keys.shape[0]
    quads = width // (4 * HDIM)
    per = CHUNK_QUADS if quads % CHUNK_QUADS == 0 else 1
    count = quads // per
    nz = n // 4
    wide = (2 * per + 1) * HDIM

    def per_chunk(slots):
        return pltpu.VMEM((count, slots, 8, wide), jnp.float32)

    dma = pltpu.SemaphoreType.DMA
    scratch = [per_chunk(n), per_chunk(n // 2)] + [per_chunk(nz)] * 5
    scratch += [
        pltpu.VMEM((tokens, width), jnp.bfloat16),
        pltpu.VMEM((tokens, width), jnp.bfloat16),
        pltpu.VMEM((16, quads * HDIM), jnp.float32),
        pltpu.VMEM((n, 16, quads * HDIM), jnp.bfloat16),
        pltpu.VMEM((count, 8, 2 * per * HDIM), jnp.float32),
        pltpu.VMEM((2 * per, n * 8, tokens), jnp.float32),
    ]
    scratch += [dma((count, 2))] + [dma((2, nz))] * 2 + [dma((nz + 1,))] * 2 + [dma((3,))] * 2
    scratch += [dma((count,))] * 4 + [dma((count, nz))] * 2
    vmem = pl.BlockSpec(memory_space=pltpu.VMEM)
    hbm = pl.BlockSpec(memory_space=pltpu.HBM)
    return pl.pallas_call(
        functools.partial(kernel, n, per),
        out_shape=jax.ShapeDtypeStruct((rows_here, width), jnp.bfloat16),
        in_specs=[vmem, hbm, hbm, vmem],
        out_specs=vmem,
        scratch_shapes=scratch,
        compiler_params=pltpu.CompilerParams(
            collective_id=0, has_side_effects=True, vmem_limit_bytes=56 * 1024 * 1024
        ),
    )(queries, keys, values, gain.reshape(1, width))


def solution(mesh):
    n = mesh.shape["seq"]
    in_specs = (P(("grp", "seq"), None), P(("grp", "seq"), None), P(("grp", "seq"), None), P())
    out_specs = P(("grp", "seq"), None)
    return jax.shard_map(
        functools.partial(shards, n), mesh=mesh, in_specs=in_specs, out_specs=out_specs, check_vma=False
    )
```

```python
import functools
import math

import jax
import jax.numpy as jnp
from jax import lax
from jax.experimental import pallas as pl
from jax.experimental.pallas import tpu as pltpu
from jax.sharding import PartitionSpec as P

HDIM = 128
CHUNKS = (2, 3, 3, 2)


def chunk_sizes(quads):
    if sum(CHUNKS) == quads:
        return CHUNKS
    return (quads,)


def remote(src, dst, send_sem, recv_sem, peer):
    return pltpu.make_async_remote_copy(
        src_ref=src,
        dst_ref=dst,
        send_sem=send_sem,
        recv_sem=recv_sem,
        device_id={"seq": peer},
        device_id_type=pl.DeviceIdType.MESH,
    )


def merge(left, right, out, pairs):
    width = pairs * HDIM
    slots = out.shape[0]
    rows = slots * 8
    stat_l = left[:, :, width:].reshape(rows, HDIM)
    stat_r = right[:, :, width:].reshape(rows, HDIM)
    peak = jnp.maximum(stat_l, stat_r)
    scale_l = jnp.exp2(stat_l - peak)
    scale_r = jnp.exp2(stat_r - peak)
    total = stat_l * pltpu.roll(scale_l, 64, 1) + stat_r * pltpu.roll(scale_r, 64, 1)
    column = lax.broadcasted_iota(jnp.int32, (rows, HDIM), 1)
    out[:, :, width:] = jnp.where(column < 64, peak, total).reshape(slots, 8, HDIM)
    for pair in range(pairs):
        at = pl.ds(pair * HDIM, HDIM)
        part_l = left[:, :, at].reshape(rows, HDIM) * scale_l[:, pair : pair + 1]
        part_r = right[:, :, at].reshape(rows, HDIM) * scale_r[:, pair : pair + 1]
        out[:, :, at] = (part_l + part_r).reshape(slots, 8, HDIM)


def kernel(n, sizes, q_ref, k_hbm, v_hbm, gain_ref, o_ref, *scratch):
    count = len(sizes)
    scratch = list(scratch)

    def take(many):
        taken = scratch[:many]
        del scratch[:many]
        return taken

    part, from_core, to_y, from_y, own, from_z = (take(count) for _ in range(6))
    k_buf, v_buf, packed, q_all, attended = take(5)
    kv_sem, gz_send, gz_recv, gy_send, gy_recv, gc_send, gc_recv = take(7)
    c_send, c_recv, y_send, y_recv, z_send, z_recv = take(6)

    nz = n // 4
    me = lax.axis_index("seq")
    z, y, core = me // 4, lax.rem(me // 2, 2), lax.rem(me, 2)
    sibling = z * 4 + y * 2 + (1 - core)
    across = z * 4 + (1 - y) * 2 + core
    offsets = list(range(1, nz))

    def z_peer(step):
        return lax.rem(z + step, nz)

    def device_at(zz):
        return zz * 4 + y * 2 + core

    starts = [sum(sizes[:i]) for i in range(count)]

    loads = []
    for i in range(count):
        columns = pl.ds(starts[i] * 4 * HDIM, sizes[i] * 4 * HDIM)
        pair = []
        for which, (hbm, buf) in enumerate(((k_hbm, k_buf), (v_hbm, v_buf))):
            copy = pltpu.make_async_copy(
                hbm.at[:, columns], buf.at[:, columns], kv_sem.at[i, which]
            )
            copy.start()
            pair.append(copy)
        loads.append(pair)

    barrier = pltpu.get_barrier_semaphore()
    for peer in [sibling, across] + [device_at(z_peer(s)) for s in offsets]:
        pl.semaphore_signal(
            barrier, inc=1, device_id={"seq": peer}, device_id_type=pl.DeviceIdType.MESH
        )

    quads = sum(sizes)
    mine = q_ref[...].astype(jnp.float32)
    for quad in range(quads):
        for j in range(4):
            head = quad * 4 + j
            packed[4 * j : 4 * j + 4, quad * HDIM : (quad + 1) * HDIM] = mine[
                :, head * HDIM : (head + 1) * HDIM
            ]
    base = core * (2 * nz) + y * nz
    other_base = core * (2 * nz) + (1 - y) * nz
    q_all[base + z] = packed[...].astype(jnp.bfloat16)

    pl.semaphore_wait(barrier, nz - 1 + 2)

    own_block = q_all.at[base + z]
    sends = []
    for s in offsets:
        to = z_peer(s)
        copy = remote(own_block, own_block, gz_send.at[to], gz_recv.at[z], device_at(to))
        copy.start()
        sends.append(copy)
    copy = remote(own_block, own_block, gy_send.at[z], gy_recv.at[z], across)
    copy.start()
    sends.append(copy)
    for s in offsets:
        src = z_peer(s)
        block = q_all.at[base + src]
        remote(block, block, gz_send.at[src], gz_recv.at[src], device_at(src)).wait_recv()
        copy = remote(block, block, gy_send.at[src], gy_recv.at[src], across)
        copy.start()
        sends.append(copy)
    near = q_all.at[pl.ds(base, nz)]
    copy = remote(near, near, gc_send.at[0], gc_recv.at[0], sibling)
    copy.start()
    sends.append(copy)
    for s in [0] + offsets:
        src = z_peer(s)
        block = q_all.at[other_base + src]
        remote(block, block, gy_send.at[src], gy_recv.at[src], across).wait_recv()
    far = q_all.at[pl.ds(other_base, nz)]
    copy = remote(far, far, gc_send.at[1], gc_recv.at[1], sibling)
    copy.start()
    sends.append(copy)
    sib_base = (1 - core) * (2 * nz)
    sib_near = q_all.at[pl.ds(sib_base + y * nz, nz)]
    sib_far = q_all.at[pl.ds(sib_base + (1 - y) * nz, nz)]
    remote(sib_near, sib_near, gc_send.at[0], gc_recv.at[0], sibling).wait_recv()
    remote(sib_far, sib_far, gc_send.at[1], gc_recv.at[1], sibling).wait_recv()

    rows = n * 8
    log_scale = math.log2(math.e) / math.sqrt(HDIM)
    first = lax.rem(lax.broadcasted_iota(jnp.int32, (rows, HDIM), 0), 8) < 4
    column = lax.broadcasted_iota(jnp.int32, (rows, HDIM), 1)

    def compute(i):
        for copy in loads[i]:
            copy.wait()
        width = sizes[i] * 2 * HDIM
        out = part[i]

        stats = jnp.zeros((rows, HDIM), jnp.float32)
        pairs = sizes[i] * 2
        columns = [pl.ds((starts[i] * 2 + pair) * 2 * HDIM, 2 * HDIM) for pair in range(pairs)]
        scores = []
        for pair in range(pairs):
            quad = starts[i] + pair // 2
            q_quad = q_all[:, :, pl.ds(quad * HDIM, HDIM)].astype(jnp.float32)
            half = pair % 2
            q_pair = q_quad[:, 8 * half : 8 * half + 8, :].reshape(rows, HDIM)
            spread = jnp.concatenate(
                [jnp.where(first, q_pair, 0.0), jnp.where(first, 0.0, q_pair)], axis=1
            ).astype(jnp.bfloat16)
            scores.append(
                lax.dot_general(
                    spread, k_buf[:, columns[pair]], (((1,), (1,)), ((), ())),
                    preferred_element_type=jnp.float32,
                )
            )
        peaks = [jnp.max(score, axis=1, keepdims=True) * log_scale for score in scores]
        weights = [jnp.exp2(score * log_scale - peak) for score, peak in zip(scores, peaks)]
        split = []
        for weight in weights:
            high = weight.astype(jnp.bfloat16)
            low = (weight - high.astype(jnp.float32)).astype(jnp.bfloat16)
            split.append(jnp.concatenate([high, low], axis=0))
        products = [
            jnp.dot(split[pair], v_buf[:, columns[pair]], preferred_element_type=jnp.float32)
            for pair in range(pairs)
        ]
        totals = [jnp.sum(weight, axis=1, keepdims=True) for weight in weights]
        for pair in range(pairs):
            summed = products[pair][:rows] + products[pair][rows:]
            picked = jnp.where(first, summed[:, :HDIM], summed[:, HDIM:])
            out[:, :, pl.ds(pair * HDIM, HDIM)] = picked.reshape(n, 8, HDIM)
            stats = jnp.where(column == pair, peaks[pair], stats)
            stats = jnp.where(column == pair + 64, totals[pair], stats)
        out[:, :, width:] = stats.reshape(n, 8, HDIM)

    def start_core(i):
        copy = remote(
            part[i].at[pl.ds((1 - core) * (2 * nz), 2 * nz)], from_core[i],
            c_send.at[i], c_recv.at[i], sibling,
        )
        copy.start()
        return copy

    def start_y(i, core_copy):
        core_copy.wait_recv()
        pairs = sizes[i] * 2
        merge(
            part[i].at[pl.ds(other_base, nz)], from_core[i].at[pl.ds((1 - y) * nz, nz)], to_y[i], pairs
        )
        copy = remote(to_y[i], from_y[i], y_send.at[i], y_recv.at[i], across)
        copy.start()
        merge(part[i].at[pl.ds(base, nz)], from_core[i].at[pl.ds(y * nz, nz)], own[i], pairs)
        return copy

    to_z = part

    def start_z(i, y_copy, core_copy):
        y_copy.wait_recv()
        core_copy.wait_send()
        there = (1 - core) * (2 * nz)
        merge(own[i], from_y[i], to_z[i].at[pl.ds(there, nz)], sizes[i] * 2)
        copies = []
        for s in offsets:
            to = z_peer(s)
            copy = remote(
                to_z[i].at[there + to], from_z[i].at[z], z_send.at[i, to], z_recv.at[i, z], device_at(to)
            )
            copy.start()
            copies.append(copy)
        from_z[i][z] = to_z[i][there + z]
        return copies

    def finish(i):
        pairs = sizes[i] * 2
        width = pairs * HDIM
        for s in offsets:
            src = z_peer(s)
            remote(
                from_z[i].at[src], from_z[i].at[src], z_send.at[i, src], z_recv.at[i, src], device_at(src)
            ).wait_recv()
        stats = from_z[i][:, :, width:]
        peak = jnp.max(stats, axis=0)
        scales = [jnp.exp2(stats[k] - peak) for k in range(nz)]
        total = sum(stats[k] * pltpu.roll(scales[k], 64, 1) for k in range(nz))
        squares = jnp.zeros((8, HDIM), jnp.float32)
        for pair in range(pairs):
            at = pl.ds(pair * HDIM, HDIM)
            numer = sum(from_z[i][k, :, at] * scales[k][:, pair : pair + 1] for k in range(nz))
            value = numer / total[:, 64 + pair : 65 + pair]
            attended[:, pl.ds((starts[i] * 2 + pair) * HDIM, HDIM)] = value
            squares = squares + value * value
        return squares

    core_copies, y_copies, z_copies = [], [], []
    for i in range(count + 2):
        if i < count:
            compute(i)
            core_copies.append(start_core(i))
        if 0 <= i - 1 < count:
            y_copies.append(start_y(i - 1, core_copies[i - 1]))
        if 0 <= i - 2 < count:
            z_copies.append(start_z(i - 2, y_copies[i - 2], core_copies[i - 2]))

    squares = sum(finish(i) for i in range(count))
    squares = squares + pltpu.roll(squares, 4, 0)
    mean = jnp.sum(squares, axis=1, keepdims=True) * (1.0 / o_ref.shape[1])
    inverse = 1.0 / jnp.sqrt(mean + 1e-06)
    for pair in range(quads * 2):
        value = attended[:, pair * HDIM : (pair + 1) * HDIM] * inverse
        for j in range(2):
            at = pl.ds((pair * 2 + j) * HDIM, HDIM)
            o_ref[:, at] = (value[4 * j : 4 * j + 4] * gain_ref[:, at]).astype(jnp.bfloat16)

    for copy in sends + y_copies:
        copy.wait_send()
    for copies in z_copies:
        for copy in copies:
            copy.wait_send()


def shards(n, queries, keys, values, gain):
    rows_here, width = queries.shape
    tokens = keys.shape[0]
    quads = width // (4 * HDIM)
    sizes = chunk_sizes(quads)
    count = len(sizes)
    nz = n // 4
    wides = [(2 * size + 1) * HDIM for size in sizes]

    def per_chunk(slots):
        return [pltpu.VMEM((slots, 8, wide), jnp.float32) for wide in wides]

    dma = pltpu.SemaphoreType.DMA
    scratch = (
        per_chunk(n) + per_chunk(n // 2) + per_chunk(nz) + per_chunk(nz) + per_chunk(nz) + per_chunk(nz)
        + [
            pltpu.VMEM((tokens, width), jnp.bfloat16),
            pltpu.VMEM((tokens, width), jnp.bfloat16),
            pltpu.VMEM((16, quads * HDIM), jnp.float32),
            pltpu.VMEM((n, 16, quads * HDIM), jnp.bfloat16),
            pltpu.VMEM((8, quads * 2 * HDIM), jnp.float32),
        ]
        + [dma((count, 2)), dma((nz,)), dma((nz,)), dma((nz,)), dma((nz,)), dma((2,)), dma((2,))]
        + [dma((count,)), dma((count,)), dma((count,)), dma((count,)), dma((count, nz)), dma((count, nz))]
    )
    vmem = pl.BlockSpec(memory_space=pltpu.VMEM)
    hbm = pl.BlockSpec(memory_space=pltpu.HBM)
    return pl.pallas_call(
        functools.partial(kernel, n, sizes),
        out_shape=jax.ShapeDtypeStruct((rows_here, width), jnp.bfloat16),
        in_specs=[vmem, hbm, hbm, vmem],
        out_specs=vmem,
        scratch_shapes=scratch,
        compiler_params=pltpu.CompilerParams(
            collective_id=0, has_side_effects=True, vmem_limit_bytes=56 * 1024 * 1024
        ),
    )(queries, keys, values, gain.reshape(1, width))


def solution(mesh):
    n = mesh.shape["seq"]
    in_specs = (P(("grp", "seq"), None), P(("grp", "seq"), None), P(("grp", "seq"), None), P())
    out_specs = P(("grp", "seq"), None)
    return jax.shard_map(
        functools.partial(shards, n), mesh=mesh, in_specs=in_specs, out_specs=out_specs, check_vma=False
    )
```
